32 devices in a mesh: dp: 8 (over z, x), mp: 4 (over y, core).
Axes of the slice: x: 2, y: 2, z: 4, core: 2. Of those that a mesh axis runs over, the one named last changes fastest.
Arguments:
- block_input: bfloat16 [8, 8192, 512], P('dp', 'mp'), may hold values from -6 to 6
- routes: int32 [8, 8192, 2], P('dp', 'mp'), may hold values from 0 to 7, all different within a row; in each aligned block of 2048 rows (0 to 2047, 2048 to 4095, ..., all dimensions but the last counted through in order) at most 1024 rows name the same one
- lengths: int32 [8], P('dp'), may hold values from 6145 to 8192, as said below
- first_gain: float32 [512], replicated, may hold values from 0.25 to 1.75
- first_bias: float32 [512], replicated, may hold values from -1.5 to 1.5
- router_weight: bfloat16 [512, 8], replicated, may hold values from -0.1875 to 0.1875
- shared_proj: bfloat16 [512, 128], replicated, may hold values from -0.25 to 0.25
- query_weight: bfloat16 [64, 4096], P('mp', 'dp'), may hold values from -0.25 to 0.25
- output_weight: bfloat16 [64, 4096], P('mp', 'dp'), may hold values from -40 to 40
- second_gain: float32 [512], replicated, may hold values from 0.25 to 1.75
- second_bias: float32 [512], replicated, may hold values from -1.5 to 1.5
- expand_weight: bfloat16 [512, 2048], P(None, 'mp'), may hold values from -0.25 to 0.25
- expand_bias: bfloat16 [2048], P('mp'), may hold values from -1.5 to 1.5
- reduce_weight: bfloat16 [2048, 512], P('mp'), may hold values from -0.125 to 0.125
- reduce_bias: bfloat16 [512], replicated, may hold values from -1.5 to 1.5
- upstream_grad: bfloat16 [8, 8192, 512], P('dp', 'mp'), may hold values from -6 to 6
Outputs:
- block_output: bfloat16 [8, 8192, 512], P('dp', 'mp')
- input_grad: float32 [8, 8192, 512], P('dp', 'mp')
- first_gain_grad: float32 [512], P('mp')
- first_bias_grad: float32 [512], P('mp')
- router_grad: float32 [512, 8], P('mp')
- shared_grad: float32 [512, 128], P('mp')
- query_weight_grad: float32 [64, 4096], P('mp', 'dp')
- output_weight_grad: float32 [64, 4096], P('mp', 'dp')
- second_gain_grad: float32 [512], P('mp')
- second_bias_grad: float32 [512], P('mp')
- expand_weight_grad: float32 [512, 2048], P(None, 'mp')
- expand_bias_grad: float32 [2048], P('mp')
- reduce_weight_grad: float32 [2048, 512], P('mp')
- reduce_bias_grad: float32 [512], P('mp')
The draws below stay inside these ranges and needn't reach their ends.
Inputs may be any that keep to these rules, and one draw needn't show every extreme that they name: `routes`: the two experts of a position differ. In each aligned block of 2048 positions of a sequence, no expert is named by more than 1024 positions, a bound that some block reaches. `lengths`: one sequence has length 8192 and another 3 * 2048 + 1.
All inputs are finite; a program needn't handle non-finite values.
Results may differ from the reference program's by a relative error of at most 0.013.
Values may be sent and summed in bfloat16 or wider, within the bound.
No kernel may reach another device: no remote copies, remote signals or barrier semaphores. Data moves between devices by JAX's collectives and lax.ppermute only.
A program may use at most 256 MiB of HBM per device.

```python
import math
import jax
import jax.numpy as jnp
import numpy as np
from jax import lax

D = 512
HEAD = 64
E = 8
FF = 2048
TOP = 2
SEQ_LEN = 8192
SEQS = 8
TOK_DEV = 2048
CAP = 1024


def draw_lengths(key, part):
    lowest = 3 * SEQ_LEN // 4 + 1
    drawn = jax.random.randint(key, (SEQS,), lowest, SEQ_LEN + 1)
    order = jax.random.permutation(jax.random.fold_in(key, 7), SEQS)
    drawn = jnp.where(order == 0, SEQ_LEN, drawn)
    drawn = jnp.where(order == 1, lowest, drawn)
    return drawn.astype(jnp.int32)


def level_of(rng, dims, cuts, smallest, largest):
    level, own = 1.0, jax.random.fold_in(rng, 6)
    for position, shards_of in cuts:
        heights = jnp.exp(jax.random.uniform(jax.random.fold_in(own, position), (shards_of,), jnp.float32, smallest / len(cuts), largest / len(cuts)))
        level = level * jnp.repeat(heights, dims[position] // shards_of).reshape([-1 if axis == position else 1 for axis in range(len(dims))])
    return level


def assign_block(own_key, own, number, rows, count, top, limit, slope):
    order = jax.random.permutation(own_key, count)
    crowded, common = portions_of(count, rows * top, limit, slope, True), portions_of(count, rows * top, limit, slope, False)
    places = jnp.arange(count)

    def named(tallies, turn):
        used = int((tallies > 0).sum())
        fixed = max(1, used // 4)
        passed = fixed + (places - fixed + turn * (used - fixed)) % max(1, count - fixed)
        return jnp.zeros((count,), jnp.int32).at[order[jnp.where(places < fixed, places, passed)]].set(jnp.asarray(tallies, jnp.int32))

    tallies = jnp.where(number % 4 == 0, named(crowded, number // 4), named(common, number - number // 4 - 1))
    mixed = jax.random.permutation(jax.random.fold_in(own, 3), count)
    giver, sink = mixed[0:count // 2 * 2:2], mixed[1:count // 2 * 2:2]
    room = jnp.minimum(tallies[giver] - 1, limit - tallies[sink]) // 2
    room = jnp.where((giver == order[0]) | (sink == order[0]) | (tallies[sink] == 0), 0, jnp.maximum(room, 0))
    passed = jax.random.randint(jax.random.fold_in(own, 4), (count // 2,), 0, 1 << 20) % (room + 1)
    tallies = tallies.at[giver].add(-passed).at[sink].add(passed)
    members = jnp.searchsorted(jnp.cumsum(tallies), jnp.arange(rows * top), side="right").astype(jnp.int32)
    listing = members.reshape(top, rows).T
    listing = listing[jax.random.permutation(jax.random.fold_in(own, 1), rows)]
    turn = jax.random.randint(jax.random.fold_in(own, 2), (rows, 1), 0, top)
    return jnp.take_along_axis(listing, (jnp.arange(top)[None, :] + turn) % top, axis=1)


def portions_of(count, total, bound, slope, full):
    loads = [(1 << 20) // math.isqrt(rank ** slope) + 1 for rank in range(1, count + 1)]
    largest = bound if full else min(bound, max(-(-total // count), total * loads[0] // sum(loads)))
    least = 1 if total - largest >= count - 1 else 0
    holding, surplus = [largest] + [least] * (count - 1), total - largest - least * (count - 1)
    while surplus > 0:
        free = [i for i in range(1, count) if holding[i] < largest] or [i for i in range(1, count) if holding[i] < bound]
        whole, left = sum([loads[i] for i in free]), surplus
        for i in free:
            addition = min(bound - holding[i], max(1, left * loads[i] // whole), surplus)
            holding[i] = holding[i] + addition
            surplus = surplus - addition
    return np.array(holding)


def noise(stream_key, shape, scale, reach, split=(), kind=jnp.bfloat16):
    values = scale * jax.random.normal(stream_key, shape, jnp.float32)
    if split:
        values = values * level_of(stream_key, shape, split, -0.22, 0.18)
    return jnp.clip(values, -reach, reach).astype(kind)


def setup_inputs(seed: int = 0) -> dict:
    key_of = jax.random.split(jax.random.key(seed), 17)
    block_input = noise(key_of[0], (SEQS, SEQ_LEN, D), 1.0, 6.0, ((0, 8), (1, 4)))
    routes_keys = jax.random.split(jax.random.fold_in(key_of[1], 1), SEQS * SEQ_LEN // TOK_DEV)
    routes_turns = jax.random.permutation(jax.random.fold_in(key_of[1], 3), SEQS * SEQ_LEN // TOK_DEV)
    routes = jax.vmap(lambda own, number: assign_block(jax.random.fold_in(key_of[1], 2), own, number, TOK_DEV, E, TOP, CAP, 1))(routes_keys, routes_turns).reshape((SEQS, SEQ_LEN, TOP))
    lengths = draw_lengths(jax.random.fold_in(key_of[16], 71), 0)
    first_gain = jnp.clip(1.0 + 0.15 * jax.random.normal(key_of[3], (D,), jnp.float32), 0.25, 1.75)
    first_bias = noise(key_of[4], (D,), 0.1, 1.5, (), jnp.float32)
    router_weight = noise(key_of[5], (D, E), (2 * D) ** -0.5, 0.1875)
    shared_proj = noise(key_of[6], (D, 2 * HEAD), D ** -0.5, 0.25)
    query_weight = noise(key_of[7], (HEAD, E * D), D ** -0.5, 0.25, ((0, 4), (1, 8)))
    output_weight = noise(key_of[8], (HEAD, E * D), (0.07 * SEQ_LEN ** 0.5), 40.0, ((0, 4), (1, 8)))
    second_gain = jnp.clip(1.0 + 0.15 * jax.random.normal(key_of[9], (D,), jnp.float32), 0.25, 1.75)
    second_bias = noise(key_of[10], (D,), 0.1, 1.5, (), jnp.float32)
    expand_weight = noise(key_of[11], (D, FF), D ** -0.5, 0.25, ((1, 4),))
    expand_bias = noise(key_of[12], (FF,), 0.1, 1.5, ((0, 4),))
    reduce_weight = noise(key_of[13], (FF, D), FF ** -0.5, 0.125, ((0, 4),))
    reduce_bias = noise(key_of[14], (D,), 0.1, 1.5)
    upstream_grad = noise(key_of[15], (SEQS, SEQ_LEN, D), 1.0, 6.0, ((0, 8), (1, 4)))
    return {"block_input": block_input, "routes": routes, "lengths": lengths, "first_gain": first_gain, "first_bias": first_bias, "router_weight": router_weight, "shared_proj": shared_proj, "query_weight": query_weight, "output_weight": output_weight, "second_gain": second_gain, "second_bias": second_bias, "expand_weight": expand_weight, "expand_bias": expand_bias, "reduce_weight": reduce_weight, "reduce_bias": reduce_bias, "upstream_grad": upstream_grad}


@jax.custom_vjp
def low(v):
    return lax.optimization_barrier(v.astype(jnp.bfloat16)).astype(jnp.float32)

@jax.custom_vjp
def low_back(v):
    return v

def low_keep(v):
    return (low(v), None)

def low_pass(kept, grad):
    return (grad,)

def back_keep(v):
    return (v, None)

def back_low(kept, grad):
    return (low(grad),)
low.defvjp(low_keep, low_pass)
low_back.defvjp(back_keep, back_low)
norm_epsilon = 1e-05
highest = lax.Precision.HIGHEST

def layer_norm(values, gain, bias):
    centred = values - lax.optimization_barrier(jnp.mean(values, axis=-1, keepdims=True))
    inverse = lax.rsqrt(lax.optimization_barrier(jnp.mean(centred * centred, axis=-1, keepdims=True)) + norm_epsilon)
    return centred * inverse * gain + bias

def gelu_tanh(values):
    return jax.nn.gelu(values, approximate=True)

def sequence_forward(params, block, route_ids, length):
    first_gain, first_bias, router_weight, shared_proj, query_weight, output_weight, second_gain, second_bias, expand_weight, expand_bias, reduce_weight, reduce_bias = params
    key_count = block.shape[0]
    width = block.shape[1]
    head_width = query_weight.shape[0]
    experts = router_weight.shape[1]
    normed = low(layer_norm(block, first_gain, first_bias))
    logits = jnp.dot(normed, router_weight, precision=highest)
    hot = (route_ids[:, :, None] == jnp.arange(experts, dtype=jnp.int32)[None, None, :]).astype(jnp.float32)
    gates = jax.nn.softmax(lax.optimization_barrier(jnp.sum(hot * logits[:, None, :], axis=-1)), axis=-1)
    pairs = low(low_back(jnp.dot(normed, shared_proj, precision=highest)))
    keys = pairs[:, :head_width]
    value_rows = pairs[:, head_width:]
    rows = low_back(jnp.broadcast_to(normed[:, None, :], (key_count, 2, width)))
    query_table = query_weight.reshape(head_width, experts, width)
    every_query = low(low_back(jnp.einsum('tsd,hed->tseh', rows, query_table, precision=highest)))
    queries = lax.optimization_barrier(jnp.sum(hot[..., None] * every_query, axis=2)).reshape(2 * key_count, head_width)
    scores = low_back(jnp.einsum('qh,kh->qk', queries, keys, precision=highest) * 0.125)
    live = jnp.arange(key_count, dtype=jnp.int32) < length
    scores = jnp.where(live[None, :], scores, -1e+30)
    attention = low(jax.nn.softmax(scores, axis=-1))
    mixed = low(low_back(jnp.dot(attention, value_rows, precision=highest)))
    per_expert = jnp.einsum('tse,tsh->teh', hot, mixed.reshape(key_count, 2, head_width), precision=highest)
    output_table = output_weight.reshape(head_width, experts, width)
    branch = low(low_back(jnp.einsum('teh,hed->ted', per_expert, output_table, precision=highest)))
    gate_table = jnp.einsum('tse,ts->te', hot, gates, precision=highest)
    middle = block + jnp.einsum('te,ted->td', gate_table, branch, precision=highest)
    normed_two = low(layer_norm(middle, second_gain, second_bias))
    expanded = low_back(jnp.dot(normed_two, expand_weight, precision=highest) + expand_bias)
    active = low(gelu_tanh(expanded))
    return middle + jnp.dot(active, reduce_weight, precision=highest) + reduce_bias

def reference(block_input, routes, lengths, first_gain, first_bias, router_weight, shared_proj, query_weight, output_weight, second_gain, second_bias, expand_weight, expand_bias, reduce_weight, reduce_bias, upstream_grad):
    params = (first_gain.astype(jnp.float32), first_bias.astype(jnp.float32), router_weight.astype(jnp.float32), shared_proj.astype(jnp.float32), query_weight.astype(jnp.float32), output_weight.astype(jnp.float32), second_gain.astype(jnp.float32), second_bias.astype(jnp.float32), expand_weight.astype(jnp.float32), expand_bias.astype(jnp.float32), reduce_weight.astype(jnp.float32), reduce_bias.astype(jnp.float32))
    source = block_input.astype(jnp.float32)

    def forward(source_all, params_all):

        def one_sequence(item):
            return sequence_forward(params_all, item[0], item[1], item[2])
        return lax.map(jax.checkpoint(one_sequence), (source_all, routes, lengths))
    result, pull = jax.vjp(forward, source, params)
    input_grad, grads = pull(upstream_grad.astype(jnp.float32))
    return (result.astype(jnp.bfloat16), input_grad, grads[0], grads[1], grads[2], grads[3], grads[4], grads[5], grads[6], grads[7], grads[8], grads[9], grads[10], grads[11])
```

```python
import functools

import jax
import jax.numpy as jnp
from jax import lax
from jax.experimental import pallas as pl
from jax.experimental.pallas import tpu as pltpu
from jax.sharding import PartitionSpec as P

F32 = jnp.float32
BF = jnp.bfloat16
EPS = 1e-05
LOG2E = 1.4426950408889634
LN2 = 0.6931471805599453
MASKED = -1e30
GELU_A = 0.7978845608028654
GELU_B = 0.044715
SAFE = 50.0
LANES = 128


def nn(a, b):
    return lax.dot_general(a, b, (((1,), (0,)), ((), ())), preferred_element_type=F32)


def nt(a, b):
    return lax.dot_general(a, b, (((1,), (1,)), ((), ())), preferred_element_type=F32)


def tn(a, b):
    return lax.dot_general(a, b, (((0,), (0,)), ((), ())), preferred_element_type=F32)


def norm_parts(values):
    centred = values - jnp.mean(values, axis=-1, keepdims=True)
    inverse = lax.rsqrt(jnp.mean(centred * centred, axis=-1, keepdims=True) + EPS)
    return centred * inverse, inverse


def norm_back(grad, normal, inverse, gain):
    scaled = grad * gain
    return inverse * (
        scaled
        - jnp.mean(scaled, axis=-1, keepdims=True)
        - normal * jnp.mean(scaled * normal, axis=-1, keepdims=True)
    )


def three(value):
    high = value.astype(BF).astype(F32)
    rest = value - high
    middle = rest.astype(BF).astype(F32)
    return high, middle, rest - middle


def extra_rows(value, last):
    row = lax.broadcasted_iota(jnp.int32, (16, value.shape[1]), 0)
    high, middle, low = three(value)
    out = jnp.where(row == 0, -high, 0.0)
    out = jnp.where(row == 1, -middle, out)
    out = jnp.where(row == 2, -low, out)
    return jnp.where(row == 3, last, out)


def spread(first, second, route0, route1, experts):
    zero = jnp.zeros_like(first)
    return jnp.concatenate(
        [
            jnp.where(route0 == e, first, jnp.where(route1 == e, second, zero))
            for e in range(experts)
        ],
        axis=0,
    )


def picked(table, route, experts):
    head = table.shape[0] // experts
    out = jnp.zeros((head, table.shape[1]), F32)
    for e in range(experts):
        out = jnp.where(route == e, table[e * head : (e + 1) * head, :], out)
    return out


def key_rows(pair, live, head):
    lane = lax.broadcasted_iota(jnp.int32, pair.shape, 1)
    row = lax.broadcasted_iota(jnp.int32, pair.shape, 0)
    ones = jnp.where(lane < head + 3, 1.0, 0.0)
    mask = jnp.where(row < live, 0.0, MASKED)
    out = jnp.where(lane == head + 3, mask, ones)
    return jnp.where(lane < head, pair.astype(F32), out).astype(BF)


def first_kernel(x, gain, bias, router, proj, routes, normed, pairs, gates):
    experts = router.shape[0] // 2
    normal, _ = norm_parts(x[...].astype(F32))
    out = (normal * gain[...] + bias[...]).astype(BF)
    normed[...] = out
    pairs[...] = nn(out, proj[...]).astype(BF)
    logits = nt(router[...], out)
    route = routes[...]
    chosen = []
    for s in range(2):
        one = jnp.zeros((1, logits.shape[1]), F32)
        for e in range(experts):
            one = jnp.where(route[s : s + 1, :] == e, logits[e : e + 1, :], one)
        chosen.append(one)
    top = jnp.maximum(chosen[0], chosen[1])
    up0, up1 = jnp.exp(chosen[0] - top), jnp.exp(chosen[1] - top)
    inverse = 1.0 / (up0 + up1)
    gates[0:1, :] = up0 * inverse
    gates[1:2, :] = up1 * inverse


def query_kernel(normed, table, routes, queries, *, experts, scale):
    every = nt(table[...], normed[...]) * scale
    for s in range(2):
        queries[s] = picked(every, routes[s : s + 1, :], experts).astype(BF)


def attend_kernel(live, q, p0, p1, p2, p3, out, keys, values, limit, top, *, head, span):
    part = p0.shape[0]

    @pl.when((pl.program_id(0) == 0) & (pl.program_id(1) == 0))
    def _():
        row = lax.broadcasted_iota(jnp.int32, (LANES, LANES), 0)
        col = lax.broadcasted_iota(jnp.int32, (LANES, LANES), 1)
        move = jnp.where((col == row + head) & (row < head), 1.0, 0.0).astype(BF)
        count = jnp.where(row < head, 1.0, 0.0).astype(BF)
        longest = jnp.zeros((1, LANES), F32)
        for o, p in enumerate((p0, p1, p2, p3)):
            pair = p[...]
            keys[o * part : (o + 1) * part, :] = key_rows(pair, live[o], head)
            turned = nt(move, pair)
            line = lax.broadcasted_iota(jnp.int32, turned.shape, 0)
            values[:, o * part : (o + 1) * part] = jnp.where(line == head, 1.0, turned).astype(BF)
            wide = pair.astype(F32)
            squares = nn((wide * wide).astype(BF), count)
            longest = jnp.maximum(longest, jnp.max(squares, axis=0, keepdims=True))
        limit[...] = jnp.broadcast_to(1.02 * jnp.sqrt(longest), limit.shape)

    query = q[0]
    wide = query.astype(F32)
    length = jnp.sqrt(jnp.sum(wide * wide, axis=0, keepdims=True))
    bound = length * limit[0:1, 0:1]
    top[...] = jnp.broadcast_to(bound, top.shape)
    n = query.shape[1]
    rest = jnp.zeros((LANES - head - 16, n), BF)

    @pl.when(jnp.max(bound) > SAFE)
    def _():
        plain = jnp.concatenate(
            [query, extra_rows(jnp.zeros((1, n), F32), 1.0).astype(BF), rest], axis=0
        )

        def peak(j, now):
            at = pl.multiple_of(j * 512, 512)
            scores = nn(keys[pl.ds(at, 512), :], plain)
            return jnp.maximum(now, jnp.max(scores, axis=0, keepdims=True))

        best = lax.fori_loop(0, 4 * part // 512, peak, jnp.full((1, n), -3e38, F32))
        top[...] = jnp.broadcast_to(best, top.shape)

    peak_row = top[0:1, :]
    extended = jnp.concatenate([query, extra_rows(peak_row, 1.0).astype(BF), rest], axis=0)
    total = jnp.zeros((LANES, n), F32)
    for j in range(4 * part // span):
        here = slice(j * span, (j + 1) * span)
        weights = jnp.exp2(nn(keys[here, :], extended)).astype(BF)
        total = total + nn(values[:, here], weights)
    weight = total[head : head + 1, :]
    out[0, 0:head, :] = total[0:head, :] / weight
    out[0, head : head + 8, :] = jnp.broadcast_to(peak_row + jnp.log2(weight), (8, n))


def attend_back_kernel(live, q, do, qt, dot, pair, before, after, grads, keys, values, kt, vt, *, head, tile):
    step = pl.program_id(0)
    part = pair.shape[0]

    @pl.when(step == 0)
    def _():
        rows = pair[...]
        keys[...] = key_rows(rows, live[0], head)
        lane = lax.broadcasted_iota(jnp.int32, rows.shape, 1)
        fixed = jnp.where(lane < 3, 1.0, 0.0)
        values[...] = jnp.where(lane < head, fixed, rows.astype(F32)).astype(BF)
        kt[...] = jnp.zeros_like(kt)
        vt[...] = jnp.zeros_like(vt)

    attention = jnp.exp2(nt(q[0], keys[...]))
    pull = nt(do[0], values[...])
    scores = (attention * pull).astype(BF)
    kt[...] += nn(qt[0], scores)
    vt[...] += nn(dot[0], attention.astype(BF))
    after[0] = before[0] + nn(scores, keys[...])

    @pl.when(step == pl.num_programs(0) - 1)
    def _():
        grads[0:head, :] = (kt[...] * LN2).astype(BF)
        grads[head : 2 * head, :] = vt[...].astype(BF)


def middle_kernel(
    att, qt, routes, gates, x, up, normed,
    we0, we1, we2, we3, eb, wr0, wr1, wr2, wr3, rb, gain, bias, wo,
    out, mid_grad, q_rows, do_rows, do_t, logit, g0, g1, g2, g3, wo_grad,
    we_sum, wr_sum, wo_sum, eb_sum, small, rt_sum,
    *, head, experts,
):
    step = pl.program_id(0)

    @pl.when(step == 0)
    def _():
        for r in (we_sum, wr_sum, wo_sum, eb_sum, small, rt_sum):
            r[...] = jnp.zeros_like(r)

    route0, route1 = routes[0:1, :], routes[1:2, :]
    gate0, gate1 = gates[0:1, :], gates[1:2, :]
    mix0, mix1 = att[0, 0:head, :], att[1, 0:head, :]
    low0, low1 = mix0.astype(BF).astype(F32), mix1.astype(BF).astype(F32)
    mixed = spread(gate0 * low0, gate1 * low1, route0, route1, experts).astype(BF)
    middle = x[...].astype(F32) + tn(mixed, wo[...])
    normal, inverse = norm_parts(middle)
    normed_two = (normal * gain[...] + bias[...]).astype(BF)
    upstream = up[...]
    n2t = normed_two.T
    upt = upstream.T
    ff = we0.shape[1]
    reduced = jnp.zeros(middle.shape, F32)
    two_grad = jnp.zeros(middle.shape, F32)
    for o, (we, wr) in enumerate(((we0, wr0), (we1, wr1), (we2, wr2), (we3, wr3))):
        here = slice(o * ff, (o + 1) * ff)
        v = nn(normed_two, we[...]) + eb[o : o + 1, :]
        square = v * v
        inner = v * (GELU_A + (GELU_A * GELU_B) * square)
        half = 0.5 + 0.5 * jnp.tanh(inner)
        act = v * half
        slope = half + 2.0 * act * (1.0 - half) * (GELU_A + (3.0 * GELU_A * GELU_B) * square)
        low = act.astype(BF)
        reduced = reduced + nn(low, wr[...])
        back = nt(upstream, wr[...]) * slope
        back_low = back.astype(BF)
        two_grad = two_grad + nt(back_low, we[...])
        we_sum[:, here] += nn(n2t, back_low)
        wr_sum[:, here] += nn(upt, low)
        eb_sum[0:1, here] += jnp.sum(back_low.astype(F32), axis=0, keepdims=True)
    out[...] = (middle + reduced + rb[...]).astype(BF)
    wide_up = upstream.astype(F32)
    mid = wide_up + norm_back(two_grad, normal, inverse, gain[...])
    mid_grad[...] = mid
    small[0:1, :] += jnp.sum(wide_up, axis=0, keepdims=True)
    small[1:2, :] += jnp.sum(two_grad * normal, axis=0, keepdims=True)
    small[2:3, :] += jnp.sum(two_grad, axis=0, keepdims=True)
    mid_low = mid.astype(BF)
    wo_sum[...] += nn(mixed, mid_low)
    every = nt(wo[...], mid_low)
    pull0, pull1 = picked(every, route0, experts), picked(every, route1, experts)
    gate_grad0 = jnp.sum(low0 * pull0, axis=0, keepdims=True)
    gate_grad1 = jnp.sum(low1 * pull1, axis=0, keepdims=True)
    both = gate0 * gate_grad0 + gate1 * gate_grad1
    chosen0, chosen1 = gate0 * (gate_grad0 - both), gate1 * (gate_grad1 - both)
    row = lax.broadcasted_iota(jnp.int32, (16, chosen0.shape[1]), 0)
    logit_rows = jnp.where(row == route0, chosen0, jnp.where(row == route1, chosen1, 0.0))
    logit_high = logit_rows.astype(BF)
    logit_low = (logit_rows - logit_high.astype(F32)).astype(BF)
    logit[...] = logit_high
    here_normed = normed[...]
    rt_sum[...] += nn(logit_high, here_normed) + nn(logit_low, here_normed)
    rest = jnp.zeros((LANES - head - 16, row.shape[1]), F32)
    for s, (gate, pull, mix) in enumerate(((gate0, pull0, mix0), (gate1, pull1, mix1))):
        grad_low = (gate * pull).astype(BF)
        do_t[s] = grad_low
        grad = grad_low.astype(F32)
        delta = jnp.sum(grad * mix, axis=0, keepdims=True)
        do_rows[s] = jnp.concatenate([extra_rows(delta, 0.0), rest, grad], axis=0).T.astype(BF)
        total = att[s, head : head + 1, :]
        query = qt[s].astype(F32)
        q_rows[s] = jnp.concatenate([query, extra_rows(total, 1.0), rest], axis=0).T.astype(BF)

    @pl.when(step == pl.num_programs(0) - 1)
    def _():
        wo_grad[...] = wo_sum[...].astype(BF)
        width = we_sum.shape[0]
        for o, g in enumerate((g0, g1, g2, g3)):
            here = slice(o * ff, (o + 1) * ff)
            g[0:width, :] = we_sum[:, here].astype(BF)
            g[width : 2 * width, :] = wr_sum[:, here].astype(BF)
            line = lax.broadcasted_iota(jnp.int32, (8, ff), 0)
            head_rows = jnp.where(line == 3, eb_sum[0:1, here], small[...])
            g[2 * width : 2 * width + 16, :] = jnp.concatenate(
                [head_rows, rt_sum[0:8, :]], axis=0
            ).astype(BF)
            g[2 * width + 16 :, :] = jnp.zeros((g.shape[0] - 2 * width - 16, ff), BF)


def last_kernel(
    where, dq, pa, pb, pc, logit, routes, normed, x, mid_grad, gain, wq, proj, router,
    out, q0, q1, q2, q3, s0, s1, s2, s3, wq_sum, sp_sum, small, *, head, experts, scale,
):
    step = pl.program_id(0)

    @pl.when(step == 0)
    def _():
        for r in (wq_sum, sp_sum, small):
            r[...] = jnp.zeros_like(r)

    route0, route1 = routes[0:1, :], routes[1:2, :]
    grad0 = (dq[0].T)[0:head, :] * scale
    grad1 = (dq[1].T)[0:head, :] * scale
    placed = spread(grad0, grad1, route0, route1, experts).astype(BF)
    pair = (pa[...].astype(F32) + pb[...].astype(F32) + pc[...].astype(F32)).astype(BF)
    normed_grad = tn(placed, wq[...]) + tn(pair, proj[...]) + tn(logit[...], router[...])
    here_normed = normed[...]
    wq_sum[...] += nn(placed, here_normed)
    sp_sum[...] += nn(pair, here_normed)
    normal, inverse = norm_parts(x[...].astype(F32))
    out[...] = mid_grad[...] + norm_back(normed_grad, normal, inverse, gain[...])
    small[0:1, :] += jnp.sum(normed_grad * normal, axis=0, keepdims=True)
    small[1:2, :] += jnp.sum(normed_grad, axis=0, keepdims=True)

    @pl.when(step == pl.num_programs(0) - 1)
    def _():
        share = head // 4
        block = sp_sum.shape[1] // 4
        for o, (q, s) in enumerate(((q0, s0), (q1, s1), (q2, s2), (q3, s3))):
            owner = where[o]
            for e in range(experts):
                at = pl.multiple_of(e * head + owner * share, share)
                q[e * share : (e + 1) * share, :] = wq_sum[pl.ds(at, share), :].astype(BF)
            lanes = pl.ds(pl.multiple_of(owner * block, block), block)
            wide = sp_sum.shape[0]
            s[0:wide, :] = sp_sum[:, lanes].astype(BF)
            s[wide : wide + 16, :] = jnp.concatenate(
                [small[:, lanes], jnp.zeros((8, block), F32)], axis=0
            ).astype(BF)


def swapped(value, bit):
    return lax.ppermute(value, "mp", [(i, i ^ bit) for i in range(4)])


def four(value):
    across = swapped(value, 2)
    return value, swapped(value, 1), across, swapped(across, 1)


def summed(a, b):
    return (a.astype(F32) + b.astype(F32)).astype(BF)


def group_sum(parts):
    far = summed(parts[2], swapped(parts[3], 1))
    near = summed(parts[0], swapped(parts[1], 1))
    return near, swapped(far, 2)


def sent_to_all(value, axes):
    n = lax.axis_size(axes)
    wide = jnp.broadcast_to(value[None], (n,) + value.shape)
    return lax.all_to_all(wide, axes, split_axis=0, concat_axis=0, tiled=True)


def whole_table(share, experts):
    dp, mp = lax.axis_size("dp"), lax.axis_size("mp")
    rows, cols = share.shape
    every = sent_to_all(share, ("dp", "mp"))
    each = every.reshape(experts, dp // experts, mp, rows, cols)
    return each.transpose(0, 2, 3, 1, 4).reshape(experts * mp * rows, dp // experts * cols)


def spec(shape, index):
    return pl.BlockSpec(shape, index)


def fixed(shape):
    return pl.BlockSpec(shape, lambda *_: (0,) * len(shape))


def shape(dims, kind):
    return jax.ShapeDtypeStruct(dims, kind)


SMEM = pl.BlockSpec(memory_space=pltpu.SMEM)
PARAMS = pltpu.CompilerParams(vmem_limit_bytes=58 * 2**20)


def on_device(
    block_input, routes, lengths, first_gain, first_bias, router_weight, shared_proj,
    query_weight, output_weight, second_gain, second_bias, expand_weight, expand_bias,
    reduce_weight, reduce_bias, upstream_grad,
):
    tokens, width = block_input.shape[1], block_input.shape[2]
    experts = router_weight.shape[1]
    head = query_weight.shape[0] * lax.axis_size("mp")
    dp = lax.axis_size("dp")
    units = expand_weight.shape[1]
    me = lax.axis_index("mp")
    owners = me ^ jnp.arange(4, dtype=jnp.int32)
    live = jnp.clip(lengths[0] - owners * tokens, 0, tokens)
    x = block_input.reshape(tokens, width)
    up = upstream_grad.reshape(tokens, width)
    routes_t = routes.reshape(tokens, 2).T
    router_t = jnp.concatenate([router_weight.T, jnp.zeros((experts, width), BF)], axis=0)
    gain1, bias1 = first_gain[None], first_bias[None]
    gain2, bias2 = second_gain[None], second_bias[None]

    wq = whole_table(query_weight, experts)

    tb = 512
    rows = spec((tb, width), lambda i: (i, 0))
    cols2 = spec((2, tb), lambda i: (0, i))
    normed, pairs, gates = pl.pallas_call(
        first_kernel,
        grid=(tokens // tb,),
        in_specs=[rows, fixed((1, width)), fixed((1, width)), fixed((2 * experts, width)),
                  fixed((width, 2 * head)), cols2],
        out_specs=[rows, spec((tb, 2 * head), lambda i: (i, 0)), cols2],
        out_shape=[shape((tokens, width), BF), shape((tokens, 2 * head), BF), shape((2, tokens), F32)],
        compiler_params=PARAMS,
    )(x, gain1, bias1, router_t, shared_proj, routes_t)

    pair = four(pairs)
    queries = pl.pallas_call(
        functools.partial(query_kernel, experts=experts, scale=0.125 * LOG2E),
        grid=(tokens // tb,),
        in_specs=[rows, fixed((experts * head, width)), cols2],
        out_specs=spec((2, head, tb), lambda i: (0, 0, i)),
        out_shape=shape((2, head, tokens), BF),
        compiler_params=PARAMS,
    )(normed, wq, routes_t)

    queries, ow, ew, rw, eb = lax.optimization_barrier(
        (queries, output_weight, expand_weight, reduce_weight, expand_bias)
    )
    wo = whole_table(ow, experts)
    wes, wrs = four(ew), four(rw)
    ebs = jnp.concatenate(four(eb[None]), axis=0).astype(F32)

    tq = 512
    att = pl.pallas_call(
        functools.partial(attend_kernel, head=head, span=4 * tokens),
        grid=(2, tokens // tq),
        in_specs=[SMEM, spec((1, head, tq), lambda s, i: (s, 0, i))] + [fixed((tokens, 2 * head))] * 4,
        out_specs=spec((1, head + 8, tq), lambda s, i: (s, 0, i)),
        out_shape=shape((2, head + 8, tokens), F32),
        scratch_shapes=[
            pltpu.VMEM((4 * tokens, LANES), BF), pltpu.VMEM((LANES, 4 * tokens), BF),
            pltpu.VMEM((8, LANES), F32), pltpu.VMEM((8, tq), F32),
        ],
        compiler_params=PARAMS,
    )(live, queries, *pair)

    tm = 256
    rows = spec((tm, width), lambda i: (i, 0))
    cols2 = spec((2, tm), lambda i: (0, i))
    tail = 1152
    both_rows = spec((2, tm, LANES), lambda i: (0, i, 0))
    both_cols = spec((2, head, tm), lambda i: (0, 0, i))
    block_out, mid_grad, q_rows, do_rows, do_t, logit, *grads = pl.pallas_call(
        functools.partial(middle_kernel, head=head, experts=experts),
        grid=(tokens // tm,),
        in_specs=[spec((2, head + 8, tm), lambda i: (0, 0, i)), both_cols, cols2, cols2, rows, rows, rows]
        + [fixed((width, units))] * 4 + [fixed((4, units))] + [fixed((units, width))] * 4
        + [fixed((1, width))] * 3 + [fixed((experts * head, width))],
        out_specs=[rows, rows, both_rows, both_rows, both_cols, spec((16, tm), lambda i: (0, i))]
        + [fixed((tail, units))] * 4 + [fixed((experts * head, width))],
        out_shape=[shape((tokens, width), BF), shape((tokens, width), F32), shape((2, tokens, LANES), BF),
                   shape((2, tokens, LANES), BF), shape((2, head, tokens), BF), shape((16, tokens), BF)]
        + [shape((tail, units), BF)] * 4 + [shape((experts * head, width), BF)],
        scratch_shapes=[
            pltpu.VMEM((width, 4 * units), F32), pltpu.VMEM((width, 4 * units), F32),
            pltpu.VMEM((experts * head, width), F32), pltpu.VMEM((8, 4 * units), F32),
            pltpu.VMEM((8, width), F32), pltpu.VMEM((16, width), F32),
        ],
        compiler_params=PARAMS,
    )(att, queries, routes_t, gates, x, up, normed, *wes, ebs, *wrs, reduce_bias[None].astype(F32),
      gain2, bias2, wo)
    *ffn_grads, wo_grad = grads

    near, far = group_sum(ffn_grads)
    own = summed(near, far).reshape(dp, tail // dp, units)
    arrived = lax.all_to_all(own, "dp", split_axis=0, concat_axis=0, tiled=True)
    piece = jnp.sum(arrived.astype(F32), axis=0).astype(BF)
    total = sent_to_all(piece, "dp").reshape(tail, units).astype(F32)

    def to_holders(grad):
        each = grad.reshape(experts, 4, head // 4, dp // experts, -1).transpose(0, 3, 1, 2, 4)
        each = each.reshape(dp * 4, head // 4, -1)
        got = lax.all_to_all(each, ("dp", "mp"), split_axis=0, concat_axis=0, tiled=True)
        return jnp.sum(got.astype(F32), axis=0)

    wo_total = to_holders(wo_grad)

    tq = 512
    key_grads = {}
    q_grad = jnp.zeros((2, tokens, LANES), F32)
    per = tokens // tq
    q_block = spec((1, tq, LANES), lambda i: (i // per, i % per, 0))
    t_block = spec((1, head, tq), lambda i: (i // per, 0, i % per))
    for o in (3, 2, 1, 0):
        q_grad, key_grads[o] = pl.pallas_call(
            functools.partial(attend_back_kernel, head=head, tile=tokens),
            grid=(2 * per,),
            in_specs=[SMEM, q_block, q_block, t_block, t_block, fixed((tokens, 2 * head)), q_block],
            out_specs=[q_block, fixed((2 * head, tokens))],
            out_shape=[shape((2, tokens, LANES), F32), shape((2 * head, tokens), BF)],
            input_output_aliases={6: 0},
            scratch_shapes=[
                pltpu.VMEM((tokens, LANES), BF), pltpu.VMEM((tokens, LANES), BF),
                pltpu.VMEM((head, tokens), F32), pltpu.VMEM((head, tokens), F32),
            ],
            compiler_params=PARAMS,
        )(live[o][None], q_rows, do_rows, queries, do_t, pair[o], q_grad)

    far = summed(key_grads[2], swapped(key_grads[3], 1))
    across = swapped(far, 2)
    beside = swapped(key_grads[1], 1)

    tl = 512
    rows = spec((tl, width), lambda i: (i, 0))
    cols2 = spec((2, tl), lambda i: (0, i))
    pair_cols = spec((2 * head, tl), lambda i: (0, i))
    share = experts * head // 4
    input_grad, *last = pl.pallas_call(
        functools.partial(last_kernel, head=head, experts=experts, scale=0.125),
        grid=(tokens // tl,),
        in_specs=[SMEM, spec((2, tl, LANES), lambda i: (0, i, 0)), pair_cols, pair_cols, pair_cols,
                  spec((16, tl), lambda i: (0, i)), cols2, rows, rows, rows, fixed((1, width)),
                  fixed((experts * head, width)), fixed((2 * head, width)), fixed((2 * experts, width))],
        out_specs=[rows] + [fixed((share, width))] * 4 + [fixed((2 * head + 16, width // 4))] * 4,
        out_shape=[shape((tokens, width), F32)] + [shape((share, width), BF)] * 4
        + [shape((2 * head + 16, width // 4), BF)] * 4,
        scratch_shapes=[
            pltpu.VMEM((experts * head, width), F32), pltpu.VMEM((2 * head, width), F32),
            pltpu.VMEM((8, width), F32),
        ],
        compiler_params=PARAMS,
    )(owners, q_grad, key_grads[0], beside, across, logit, routes_t, normed, x, mid_grad, gain1, wq,
      shared_proj.T, router_t)

    near, far = group_sum(last[:4])
    mine = summed(near, far).reshape(experts, head // 4, dp // experts, -1).transpose(0, 2, 1, 3)
    mine = mine.reshape(dp, head // 4, -1)
    got = lax.all_to_all(mine, "dp", split_axis=0, concat_axis=0, tiled=True)
    wq_total = jnp.sum(got.astype(F32), axis=0)
    near, far = group_sum(last[4:])
    ends = jnp.sum(sent_to_all(summed(near, far), "dp").astype(F32), axis=0)

    block = width // 4
    cut = lax.dynamic_slice_in_dim(total[2 * width : 2 * width + 16], me * block, block, axis=1)
    return (
        block_out.reshape(1, tokens, width),
        input_grad.reshape(1, tokens, width),
        ends[2 * head],
        ends[2 * head + 1],
        cut[8 : 8 + experts].T,
        ends[: 2 * head].T,
        wq_total,
        wo_total,
        cut[1],
        cut[2],
        total[:width],
        total[2 * width + 3],
        total[width : 2 * width].T,
        cut[0],
    )


def solution(mesh):
    both = P("dp", "mp", None)
    table = P("mp", "dp")
    placed = (
        both, both, P("dp"), P(), P(), P(), P(), table, table, P(), P(), P(None, "mp"), P("mp"),
        P("mp", None), P(), both,
    )
    given = (
        both, both, P("mp"), P("mp"), P("mp", None), P("mp", None), table, table, P("mp"), P("mp"),
        P(None, "mp"), P("mp"), P("mp", None), P("mp"),
    )
    return jax.shard_map(on_device, mesh=mesh, in_specs=placed, out_specs=given, check_vma=False)
```

```python
import functools

import jax
import jax.numpy as jnp
from jax import lax
from jax.experimental import pallas as pl
from jax.experimental.pallas import tpu as pltpu
from jax.sharding import PartitionSpec as P

F32 = jnp.float32
BF = jnp.bfloat16
EPS = 1e-05
LOG2E = 1.4426950408889634
LN2 = 0.6931471805599453
MASKED = -1e30
GELU_A = 0.7978845608028654
GELU_B = 0.044715
SAFE = 50.0
LANES = 128


def nn(a, b):
    return lax.dot_general(a, b, (((1,), (0,)), ((), ())), preferred_element_type=F32)


def nt(a, b):
    return lax.dot_general(a, b, (((1,), (1,)), ((), ())), preferred_element_type=F32)


def tn(a, b):
    return lax.dot_general(a, b, (((0,), (0,)), ((), ())), preferred_element_type=F32)


def norm_parts(values):
    centred = values - jnp.mean(values, axis=-1, keepdims=True)
    inverse = lax.rsqrt(jnp.mean(centred * centred, axis=-1, keepdims=True) + EPS)
    return centred * inverse, inverse


def norm_back(grad, normal, inverse, gain):
    scaled = grad * gain
    return inverse * (
        scaled
        - jnp.mean(scaled, axis=-1, keepdims=True)
        - normal * jnp.mean(scaled * normal, axis=-1, keepdims=True)
    )


def three(value):
    high = value.astype(BF).astype(F32)
    rest = value - high
    middle = rest.astype(BF).astype(F32)
    return high, middle, rest - middle


def extra_rows(value, last):
    row = lax.broadcasted_iota(jnp.int32, (16, value.shape[1]), 0)
    high, middle, low = three(value)
    out = jnp.where(row == 0, -high, 0.0)
    out = jnp.where(row == 1, -middle, out)
    out = jnp.where(row == 2, -low, out)
    return jnp.where(row == 3, last, out)


def spread(first, second, route0, route1, experts):
    zero = jnp.zeros_like(first)
    return jnp.concatenate(
        [
            jnp.where(route0 == e, first, jnp.where(route1 == e, second, zero))
            for e in range(experts)
        ],
        axis=0,
    )


def picked(table, route, experts):
    head = table.shape[0] // experts
    out = jnp.zeros((head, table.shape[1]), F32)
    for e in range(experts):
        out = jnp.where(route == e, table[e * head : (e + 1) * head, :], out)
    return out


def key_rows(pair, live, head):
    lane = lax.broadcasted_iota(jnp.int32, pair.shape, 1)
    row = lax.broadcasted_iota(jnp.int32, pair.shape, 0)
    ones = jnp.where(lane < head + 3, 1.0, 0.0)
    mask = jnp.where(row < live, 0.0, MASKED)
    out = jnp.where(lane == head + 3, mask, ones)
    return jnp.where(lane < head, pair.astype(F32), out).astype(BF)


def first_kernel(x, gain, bias, router, proj, routes, normed, pairs, gates):
    experts = router.shape[0] // 2
    normal, _ = norm_parts(x[...].astype(F32))
    out = (normal * gain[...] + bias[...]).astype(BF)
    normed[...] = out
    pairs[...] = nn(out, proj[...]).astype(BF)
    logits = nt(router[...], out)
    route = routes[...]
    chosen = []
    for s in range(2):
        one = jnp.zeros((1, logits.shape[1]), F32)
        for e in range(experts):
            one = jnp.where(route[s : s + 1, :] == e, logits[e : e + 1, :], one)
        chosen.append(one)
    top = jnp.maximum(chosen[0], chosen[1])
    up0, up1 = jnp.exp(chosen[0] - top), jnp.exp(chosen[1] - top)
    inverse = 1.0 / (up0 + up1)
    gates[0:1, :] = up0 * inverse
    gates[1:2, :] = up1 * inverse


def query_kernel(normed, table, routes, queries, *, experts, scale):
    every = nt(table[...], normed[...]) * scale
    for s in range(2):
        queries[s] = picked(every, routes[s : s + 1, :], experts).astype(BF)


def attend_kernel(live, q, p0, p1, p2, p3, out, keys, values, limit, top, *, head, span):
    part = p0.shape[0]

    @pl.when((pl.program_id(0) == 0) & (pl.program_id(1) == 0))
    def _():
        row = lax.broadcasted_iota(jnp.int32, (LANES, LANES), 0)
        col = lax.broadcasted_iota(jnp.int32, (LANES, LANES), 1)
        move = jnp.where((col == row + head) & (row < head), 1.0, 0.0).astype(BF)
        count = jnp.where(row < head, 1.0, 0.0).astype(BF)
        longest = jnp.zeros((1, LANES), F32)
        for o, p in enumerate((p0, p1, p2, p3)):
            pair = p[...]
            keys[o * part : (o + 1) * part, :] = key_rows(pair, live[o], head)
            turned = nt(move, pair)
            line = lax.broadcasted_iota(jnp.int32, turned.shape, 0)
            values[:, o * part : (o + 1) * part] = jnp.where(line == head, 1.0, turned).astype(BF)
            wide = pair.astype(F32)
            squares = nn((wide * wide).astype(BF), count)
            longest = jnp.maximum(longest, jnp.max(squares, axis=0, keepdims=True))
        limit[...] = jnp.broadcast_to(1.02 * jnp.sqrt(longest), limit.shape)

    query = q[0]
    wide = query.astype(F32)
    length = jnp.sqrt(jnp.sum(wide * wide, axis=0, keepdims=True))
    bound = length * limit[0:1, 0:1]
    top[...] = jnp.broadcast_to(bound, top.shape)
    n = query.shape[1]
    rest = jnp.zeros((LANES - head - 16, n), BF)

    @pl.when(jnp.max(bound) > SAFE)
    def _():
        plain = jnp.concatenate(
            [query, extra_rows(jnp.zeros((1, n), F32), 1.0).astype(BF), rest], axis=0
        )

        def peak(j, now):
            at = pl.multiple_of(j * 512, 512)
            scores = nn(keys[pl.ds(at, 512), :], plain)
            return jnp.maximum(now, jnp.max(scores, axis=0, keepdims=True))

        best = lax.fori_loop(0, 4 * part // 512, peak, jnp.full((1, n), -3e38, F32))
        top[...] = jnp.broadcast_to(best, top.shape)

    peak_row = top[0:1, :]
    extended = jnp.concatenate([query, extra_rows(peak_row, 1.0).astype(BF), rest], axis=0)
    total = jnp.zeros((LANES, n), F32)
    for j in range(4 * part // span):
        here = slice(j * span, (j + 1) * span)
        weights = jnp.exp2(nn(keys[here, :], extended)).astype(BF)
        total = total + nn(values[:, here], weights)
    weight = total[head : head + 1, :]
    out[0, 0:head, :] = total[0:head, :] / weight
    out[0, head : head + 8, :] = jnp.broadcast_to(peak_row + jnp.log2(weight), (8, n))


def attend_back_kernel(live, q, do, qt, dot, before, *rest, head, pieces):
    pairs, after = rest[:pieces], rest[pieces]
    grads = rest[pieces + 1 : 2 * pieces + 1]
    keys, values, kt, vt = rest[2 * pieces + 1 :]
    step = pl.program_id(0)
    size = pairs[0].shape[0]

    @pl.when(step == 0)
    def _():
        for n, pair in enumerate(pairs):
            here = slice(n * size, (n + 1) * size)
            rows = pair[...]
            keys[here, :] = key_rows(rows, live[n], head)
            lane = lax.broadcasted_iota(jnp.int32, rows.shape, 1)
            fixed = jnp.where(lane < 3, 1.0, 0.0)
            values[here, :] = jnp.where(lane < head, fixed, rows.astype(F32)).astype(BF)
        kt[...] = jnp.zeros_like(kt)
        vt[...] = jnp.zeros_like(vt)

    attention = jnp.exp2(nt(q[0], keys[...]))
    pull = nt(do[0], values[...])
    scores = (attention * pull).astype(BF)
    kt[...] += nn(qt[0], scores)
    vt[...] += nn(dot[0], attention.astype(BF))
    after[0] = before[0] + nn(scores, keys[...])

    @pl.when(step == pl.num_programs(0) - 1)
    def _():
        for n, grad in enumerate(grads):
            here = slice(n * size, (n + 1) * size)
            grad[0:head, :] = (kt[:, here] * LN2).astype(BF)
            grad[head : 2 * head, :] = vt[:, here].astype(BF)


def middle_kernel(
    where, att0, att1, qt, routes, gates, x, up, normed,
    w0, w1, w2, w3, rb, gain, bias, wo,
    out, mid_grad, q_rows, do_rows, do_t, logit, g0, g1, g2, g3,
    we_sum, wr_sum, wo_sum, eb_sum, small, rt_sum,
    *, head, experts,
):
    step = pl.program_id(0)

    @pl.when(step == 0)
    def _():
        for r in (we_sum, wr_sum, wo_sum, eb_sum, small, rt_sum):
            r[...] = jnp.zeros_like(r)

    route0, route1 = routes[0:1, :], routes[1:2, :]
    gate0, gate1 = gates[0:1, :], gates[1:2, :]
    mix0, mix1 = att0[0, 0:head, :], att1[0, 0:head, :]
    low0, low1 = mix0.astype(BF).astype(F32), mix1.astype(BF).astype(F32)
    mixed = spread(gate0 * low0, gate1 * low1, route0, route1, experts).astype(BF)
    middle = x[...].astype(F32) + tn(mixed, wo[...])
    normal, inverse = norm_parts(middle)
    normed_two = (normal * gain[...] + bias[...]).astype(BF)
    upstream = up[...]
    n2t = normed_two.T
    upt = upstream.T
    ff = w0.shape[1]
    width = middle.shape[1]
    reduced = jnp.zeros(middle.shape, F32)
    two_grad = jnp.zeros(middle.shape, F32)
    for o, w in enumerate((w0, w1, w2, w3)):
        here = slice(o * ff, (o + 1) * ff)
        we, wr = w[0:width, :], w[width : width + ff, :]
        v = nn(normed_two, we) + w[width + ff : width + ff + 16, :].astype(F32)[0:1, :]
        square = v * v
        inner = v * (GELU_A + (GELU_A * GELU_B) * square)
        half = 0.5 + 0.5 * jnp.tanh(inner)
        act = v * half
        slope = half + 2.0 * act * (1.0 - half) * (GELU_A + (3.0 * GELU_A * GELU_B) * square)
        low = act.astype(BF)
        reduced = reduced + nn(low, wr)
        back = nt(upstream, wr) * slope
        back_low = back.astype(BF)
        two_grad = two_grad + nt(back_low, we)
        we_sum[:, here] += nn(n2t, back_low)
        wr_sum[:, here] += nn(upt, low)
        eb_sum[0:1, here] += jnp.sum(back_low.astype(F32), axis=0, keepdims=True)
    out[...] = (middle + reduced + rb[...]).astype(BF)
    wide_up = upstream.astype(F32)
    mid = wide_up + norm_back(two_grad, normal, inverse, gain[...])
    mid_grad[...] = mid
    small[0:1, :] += jnp.sum(wide_up, axis=0, keepdims=True)
    small[1:2, :] += jnp.sum(two_grad * normal, axis=0, keepdims=True)
    small[2:3, :] += jnp.sum(two_grad, axis=0, keepdims=True)
    mid_low = mid.astype(BF)
    wo_sum[...] += nn(mixed, mid_low)
    every = nt(wo[...], mid_low)
    pull0, pull1 = picked(every, route0, experts), picked(every, route1, experts)
    gate_grad0 = jnp.sum(low0 * pull0, axis=0, keepdims=True)
    gate_grad1 = jnp.sum(low1 * pull1, axis=0, keepdims=True)
    both = gate0 * gate_grad0 + gate1 * gate_grad1
    chosen0, chosen1 = gate0 * (gate_grad0 - both), gate1 * (gate_grad1 - both)
    row = lax.broadcasted_iota(jnp.int32, (16, chosen0.shape[1]), 0)
    logit_rows = jnp.where(row == route0, chosen0, jnp.where(row == route1, chosen1, 0.0))
    logit_high = logit_rows.astype(BF)
    logit_low = (logit_rows - logit_high.astype(F32)).astype(BF)
    logit[...] = logit_high
    here_normed = normed[...]
    rt_sum[...] += nn(logit_high, here_normed) + nn(logit_low, here_normed)
    rest = jnp.zeros((LANES - head - 16, row.shape[1]), F32)
    for s, (gate, pull, mix, att) in enumerate(
        ((gate0, pull0, mix0, att0), (gate1, pull1, mix1, att1))
    ):
        grad_low = (gate * pull).astype(BF)
        do_t[s] = grad_low
        grad = grad_low.astype(F32)
        delta = jnp.sum(grad * mix, axis=0, keepdims=True)
        do_rows[s] = jnp.concatenate([extra_rows(delta, 0.0), rest, grad], axis=0).T.astype(BF)
        total = att[0, head : head + 1, :]
        query = qt[s].astype(F32)
        q_rows[s] = jnp.concatenate([query, extra_rows(total, 1.0), rest], axis=0).T.astype(BF)

    @pl.when(step == pl.num_programs(0) - 1)
    def _():
        share = head // 4
        table = g0.shape[0] - experts * share
        for o, g in enumerate((g0, g1, g2, g3)):
            here = slice(o * ff, (o + 1) * ff)
            g[0:width, :] = we_sum[:, here].astype(BF)
            g[width : 2 * width, :] = wr_sum[:, here].astype(BF)
            line = lax.broadcasted_iota(jnp.int32, (8, ff), 0)
            head_rows = jnp.where(line == 3, eb_sum[0:1, here], small[...])
            g[2 * width : 2 * width + 16, :] = jnp.concatenate(
                [head_rows, rt_sum[0:8, :]], axis=0
            ).astype(BF)
            g[2 * width + 16 : table, :] = jnp.zeros((table - 2 * width - 16, ff), BF)
            for e in range(experts):
                at = pl.multiple_of(e * head + where[o] * share, share)
                g[table + e * share : table + (e + 1) * share, :] = wo_sum[
                    pl.ds(at, share), :
                ].astype(BF)


def last_kernel(
    where, dq, pa, pd, pb, pc, logit, routes, normed, x, mid_grad, gain, wq, proj, router,
    out, s0, s1, s2, s3, wq_sum, sp_sum, small, *, head, experts, scale,
):
    step = pl.program_id(0)

    @pl.when(step == 0)
    def _():
        for r in (wq_sum, sp_sum, small):
            r[...] = jnp.zeros_like(r)

    route0, route1 = routes[0:1, :], routes[1:2, :]
    grad0 = (dq[0].T)[0:head, :] * scale
    grad1 = (dq[1].T)[0:head, :] * scale
    placed = spread(grad0, grad1, route0, route1, experts).astype(BF)
    own = jnp.where(step < pl.num_programs(0) // 2, pa[...].astype(F32), pd[...].astype(F32))
    pair = (own + pb[...].astype(F32) + pc[...].astype(F32)).astype(BF)
    normed_grad = tn(placed, wq[...]) + tn(pair, proj[...]) + tn(logit[...], router[...])
    here_normed = normed[...]
    wq_sum[...] += nn(placed, here_normed)
    sp_sum[...] += nn(pair, here_normed)
    normal, inverse = norm_parts(x[...].astype(F32))
    out[...] = mid_grad[...] + norm_back(normed_grad, normal, inverse, gain[...])
    small[0:1, :] += jnp.sum(normed_grad * normal, axis=0, keepdims=True)
    small[1:2, :] += jnp.sum(normed_grad, axis=0, keepdims=True)

    @pl.when(step == pl.num_programs(0) - 1)
    def _():
        share = head // 4
        block = sp_sum.shape[1] // 4
        each = sp_sum.shape[0] // 4
        table = experts * share
        for o, s in enumerate((s0, s1, s2, s3)):
            owner = where[o]
            for e in range(experts):
                at = pl.multiple_of(e * head + owner * share, share)
                s[e * share : (e + 1) * share, :] = wq_sum[pl.ds(at, share), :].astype(BF)
            lanes = pl.ds(pl.multiple_of(owner * block, block), block)
            s[table + each : table + each + 16, :] = jnp.zeros((16, 4 * block), BF)
            ends = jnp.concatenate([small[:, lanes], jnp.zeros((8, block), F32)], axis=0)
            s[table + each : table + each + 16, 0:block] = ends.astype(BF)
            for g in range(4):
                piece = sp_sum[g * each : (g + 1) * each, lanes]
                s[table : table + each, g * block : (g + 1) * block] = piece.astype(BF)


def swapped(value, bit):
    return lax.ppermute(value, "mp", [(i, i ^ bit) for i in range(4)])


def four(value):
    across = swapped(value, 2)
    return value, swapped(value, 1), across, swapped(across, 1)


def summed(a, b):
    return (a.astype(F32) + b.astype(F32)).astype(BF)


def group_sum(parts):
    far = summed(parts[2], swapped(parts[3], 1))
    near = summed(parts[0], swapped(parts[1], 1))
    return near, swapped(far, 2)


def sent_to_all(value, axes):
    n = lax.axis_size(axes)
    wide = jnp.broadcast_to(value[None], (n,) + value.shape)
    return lax.all_to_all(wide, axes, split_axis=0, concat_axis=0, tiled=True)


def whole_table(share, experts):
    dp, mp = lax.axis_size("dp"), lax.axis_size("mp")
    rows, cols = share.shape
    every = sent_to_all(share, ("dp", "mp"))
    each = every.reshape(experts, dp // experts, mp, rows, cols)
    return each.transpose(0, 2, 3, 1, 4).reshape(experts * mp * rows, dp // experts * cols)


def spec(shape, index):
    return pl.BlockSpec(shape, index)


def fixed(shape):
    return pl.BlockSpec(shape, lambda *_: (0,) * len(shape))


def shape(dims, kind):
    return jax.ShapeDtypeStruct(dims, kind)


SMEM = pl.BlockSpec(memory_space=pltpu.SMEM)
PARAMS = pltpu.CompilerParams(vmem_limit_bytes=58 * 2**20)


def cost(us):
    return pl.CostEstimate(flops=int(us * 1.1e9), bytes_accessed=1024, transcendentals=0)


def tied(value, *others):
    return lax.optimization_barrier((value, *others))[0]


def on_device(
    block_input, routes, lengths, first_gain, first_bias, router_weight, shared_proj,
    query_weight, output_weight, second_gain, second_bias, expand_weight, expand_bias,
    reduce_weight, reduce_bias, upstream_grad,
):
    tokens, width = block_input.shape[1], block_input.shape[2]
    experts = router_weight.shape[1]
    head = query_weight.shape[0] * lax.axis_size("mp")
    dp = lax.axis_size("dp")
    units = expand_weight.shape[1]
    me = lax.axis_index("mp")
    owners = me ^ jnp.arange(4, dtype=jnp.int32)
    live = jnp.clip(lengths[0] - owners * tokens, 0, tokens)
    x = block_input.reshape(tokens, width)
    up = upstream_grad.reshape(tokens, width)
    routes_t = routes.reshape(tokens, 2).T
    router_t = jnp.concatenate([router_weight.T, jnp.zeros((experts, width), BF)], axis=0)
    gain1, bias1 = first_gain[None], first_bias[None]
    gain2, bias2 = second_gain[None], second_bias[None]

    feed = jnp.concatenate(
        [expand_weight, reduce_weight, jnp.broadcast_to(expand_bias[None], (16, units))], axis=0
    )
    wq = whole_table(query_weight, experts)

    tb = 512
    rows = spec((tb, width), lambda i: (i, 0))
    cols2 = spec((2, tb), lambda i: (0, i))
    normed, pairs, gates = pl.pallas_call(
        first_kernel,
        grid=(tokens // tb,),
        in_specs=[rows, fixed((1, width)), fixed((1, width)), fixed((2 * experts, width)),
                  fixed((width, 2 * head)), cols2],
        out_specs=[rows, spec((tb, 2 * head), lambda i: (i, 0)), cols2],
        out_shape=[shape((tokens, width), BF), shape((tokens, 2 * head), BF), shape((2, tokens), F32)],
        compiler_params=PARAMS,
        cost_estimate=cost(5),
    )(x, gain1, bias1, router_t, shared_proj, routes_t)

    pair_across = swapped(pairs, 2)
    pair_beside = swapped(pairs, 1)
    queries = pl.pallas_call(
        functools.partial(query_kernel, experts=experts, scale=0.125 * LOG2E),
        grid=(tokens // tb,),
        in_specs=[rows, fixed((experts * head, width)), cols2],
        out_specs=spec((2, head, tb), lambda i: (0, 0, i)),
        out_shape=shape((2, head, tokens), BF),
        compiler_params=PARAMS,
        cost_estimate=cost(5),
    )(normed, wq, routes_t)
    feed, pair_across, queries = lax.optimization_barrier((feed, pair_across, queries))
    feed_across = swapped(feed, 2)
    feed_beside = swapped(feed, 1)
    pair = (pairs, pair_beside, pair_across, swapped(pair_across, 1))
    wo = whole_table(tied(output_weight, queries), experts)

    tq = 512
    calls = []
    for s in range(2):
        if s == 1:
            queries, feed_across = lax.optimization_barrier((queries, feed_across))
        calls.append(pl.pallas_call(
            functools.partial(attend_kernel, head=head, span=4 * tokens),
            grid=(1, tokens // tq),
            in_specs=[SMEM, spec((1, head, tq), lambda _, i, s=s: (s, 0, i))]
            + [fixed((tokens, 2 * head))] * 4,
            out_specs=spec((1, head + 8, tq), lambda s, i: (s, 0, i)),
            out_shape=shape((1, head + 8, tokens), F32),
            scratch_shapes=[
                pltpu.VMEM((4 * tokens, LANES), BF), pltpu.VMEM((LANES, 4 * tokens), BF),
                pltpu.VMEM((8, LANES), F32), pltpu.VMEM((8, tq), F32),
            ],
            compiler_params=PARAMS,
            cost_estimate=cost(17),
        )(live, queries, *pair))
    feeds = (feed, feed_beside, feed_across, swapped(feed_across, 1))

    tm = 512
    rows = spec((tm, width), lambda i: (i, 0))
    cols2 = spec((2, tm), lambda i: (0, i))
    tail = 2 * width + 64
    share = experts * head // 4
    slot = tail + share
    both_rows = spec((2, tm, LANES), lambda i: (0, i, 0))
    both_cols = spec((2, head, tm), lambda i: (0, 0, i))
    att_cols = spec((1, head + 8, tm), lambda i: (0, 0, i))
    block_out, mid_grad, q_rows, do_rows, do_t, logit, *ffn = pl.pallas_call(
        functools.partial(middle_kernel, head=head, experts=experts),
        grid=(tokens // tm,),
        in_specs=[SMEM, att_cols, att_cols, both_cols, cols2, cols2, rows, rows, rows]
        + [fixed((width + units + 16, units))] * 4
        + [fixed((1, width))] * 3 + [fixed((experts * head, width))],
        out_specs=[rows, rows, both_rows, both_rows, both_cols, spec((16, tm), lambda i: (0, i))]
        + [fixed((slot, units))] * 4,
        out_shape=[shape((tokens, width), BF), shape((tokens, width), F32), shape((2, tokens, LANES), BF),
                   shape((2, tokens, LANES), BF), shape((2, head, tokens), BF), shape((16, tokens), BF)]
        + [shape((slot, units), BF)] * 4,
        scratch_shapes=[
            pltpu.VMEM((width, 4 * units), F32), pltpu.VMEM((width, 4 * units), F32),
            pltpu.VMEM((experts * head, width), F32), pltpu.VMEM((8, 4 * units), F32),
            pltpu.VMEM((8, width), F32), pltpu.VMEM((16, width), F32),
        ],
        compiler_params=PARAMS,
        cost_estimate=cost(50),
    )(owners, *calls, queries, routes_t, gates, x, up, normed, *feeds, reduce_bias[None].astype(F32),
      gain2, bias2, wo)

    tq = 1024
    per = tokens // tq
    q_block = spec((1, tq, LANES), lambda i: (i // per, i % per, 0))
    t_block = spec((1, head, tq), lambda i: (i // per, 0, i % per))

    def back_call(places, size, before, us):
        parts = len(places)
        keep = jnp.stack([live[o] - at * size for o, at in places])
        many = parts * size
        return pl.pallas_call(
            functools.partial(attend_back_kernel, head=head, pieces=parts),
            grid=(2 * per,),
            in_specs=[SMEM, q_block, q_block, t_block, t_block, q_block]
            + [spec((size, 2 * head), lambda i, at=at: (at, 0)) for _, at in places],
            out_specs=[q_block] + [fixed((2 * head, size))] * parts,
            out_shape=[shape((2, tokens, LANES), F32)] + [shape((2 * head, size), BF)] * parts,
            input_output_aliases={5: 0},
            scratch_shapes=[
                pltpu.VMEM((many, LANES), BF), pltpu.VMEM((many, LANES), BF),
                pltpu.VMEM((head, many), F32), pltpu.VMEM((head, many), F32),
            ],
            compiler_params=PARAMS,
            cost_estimate=cost(us),
        )(keep, q_rows, do_rows, queries, do_t, before, *[pair[o] for o, _ in places])

    def by_holder(rows_of):
        each = rows_of.reshape(experts, head // 4, dp // experts, -1).transpose(0, 2, 1, 3)
        return each.reshape(dp, -1, width)

    half = tokens // 2
    from3, from1 = swapped(ffn[3], 1), swapped(ffn[1], 1)
    q_grad = jnp.zeros((2, tokens, LANES), F32)
    q_grad, key0a = back_call([(0, 0)], half, q_grad, 12)
    far, near = summed(ffn[2], from3), summed(ffn[0], from1)
    q_grad, far, near = lax.optimization_barrier((q_grad, far, near))
    from2 = swapped(far, 2)
    q_grad, key3 = back_call([(3, 0)], tokens, q_grad, 24)
    key_from3 = swapped(key3, 1)
    own = summed(near, from2)
    own = jnp.concatenate([own[:tail].reshape(dp, -1, width), by_holder(own[tail:])], axis=1)
    q_grad, own = lax.optimization_barrier((q_grad, own))
    arrived = lax.all_to_all(own, "dp", split_axis=0, concat_axis=0, tiled=True)
    q_grad, key2, key1 = back_call([(2, 0), (1, 0)], tokens, q_grad, 47)
    key_far = summed(key2, key_from3)
    piece = jnp.sum(arrived.astype(F32), axis=0)
    q_grad, piece, key_far = lax.optimization_barrier((q_grad, piece, key_far))
    beside = swapped(key1, 1)
    across = swapped(key_far, 2)
    total = sent_to_all(piece[: tail // dp].astype(BF), "dp").reshape(tail, units)
    wo_total = piece[tail // dp :].reshape(head // 4, -1)
    q_grad, key0b = back_call([(0, 1)], half, q_grad, 12)

    tl = 512
    rows = spec((tl, width), lambda i: (i, 0))
    cols2 = spec((2, tl), lambda i: (0, i))
    pair_cols = spec((2 * head, tl), lambda i: (0, i))
    count = half // tl
    first_cols = spec((2 * head, tl), lambda i: (0, jnp.minimum(i, count - 1)))
    second_cols = spec((2 * head, tl), lambda i: (0, jnp.maximum(i - count, 0)))
    input_grad, *last = pl.pallas_call(
        functools.partial(last_kernel, head=head, experts=experts, scale=0.125),
        grid=(tokens // tl,),
        in_specs=[SMEM, spec((2, tl, LANES), lambda i: (0, i, 0)), first_cols, second_cols, pair_cols, pair_cols,
                  spec((16, tl), lambda i: (0, i)), cols2, rows, rows, rows, fixed((1, width)),
                  fixed((experts * head, width)), fixed((2 * head, width)), fixed((2 * experts, width))],
        out_specs=[rows] + [fixed((share + 48, width))] * 4,
        out_shape=[shape((tokens, width), F32)] + [shape((share + 48, width), BF)] * 4,
        scratch_shapes=[
            pltpu.VMEM((experts * head, width), F32), pltpu.VMEM((2 * head, width), F32),
            pltpu.VMEM((8, width), F32),
        ],
        compiler_params=PARAMS,
        cost_estimate=cost(10),
    )(owners, q_grad, key0a, key0b, beside, across, logit, routes_t, normed, x, mid_grad, gain1, wq,
      shared_proj.T, router_t)

    near, far = group_sum(last)
    mine, total = lax.optimization_barrier((summed(near, far), total))
    total = total.astype(F32)
    ends = jnp.broadcast_to(mine[share:][None], (dp, 48, width))
    each = jnp.concatenate([by_holder(mine[:share]), ends], axis=1)
    got = lax.all_to_all(each, "dp", split_axis=0, concat_axis=0, tiled=True)
    got = jnp.sum(got.astype(F32), axis=0)
    wq_total = got[: share // dp].reshape(head // 4, -1)
    ends = got[share // dp :]
    block = width // 4
    each = 2 * head // 4
    shared_total = jnp.concatenate(
        [ends[:each, g * block : (g + 1) * block] for g in range(4)], axis=0
    )
    cut = lax.dynamic_slice_in_dim(total[2 * width : 2 * width + 16], me * block, block, axis=1)
    return (
        block_out.reshape(1, tokens, width),
        input_grad.reshape(1, tokens, width),
        ends[each, :block],
        ends[each + 1, :block],
        cut[8 : 8 + experts].T,
        shared_total.T,
        wq_total,
        wo_total,
        cut[1],
        cut[2],
        total[:width],
        total[2 * width + 3],
        total[width : 2 * width].T,
        cut[0],
    )


def solution(mesh):
    both = P("dp", "mp", None)
    table = P("mp", "dp")
    placed = (
        both, both, P("dp"), P(), P(), P(), P(), table, table, P(), P(), P(None, "mp"), P("mp"),
        P("mp", None), P(), both,
    )
    given = (
        both, both, P("mp"), P("mp"), P("mp", None), P("mp", None), table, table, P("mp"), P("mp"),
        P(None, "mp"), P("mp"), P("mp", None), P("mp"),
    )
    return jax.shard_map(on_device, mesh=mesh, in_specs=placed, out_specs=given, check_vma=False)
```

```python
import functools

import jax
import jax.numpy as jnp
from jax import lax
from jax.experimental import pallas as pl
from jax.experimental.pallas import tpu as pltpu
from jax.sharding import PartitionSpec as P

F32 = jnp.float32
BF = jnp.bfloat16
EPS = 1e-05
LOG2E = 1.4426950408889634
LN2 = 0.6931471805599453
MASKED = -1e30
GELU_A = 0.7978845608028654
GELU_B = 0.044715
SAFE = 60.0
LANES = 128


def nn(a, b):
    return lax.dot_general(a, b, (((1,), (0,)), ((), ())), preferred_element_type=F32)


def nt(a, b):
    return lax.dot_general(a, b, (((1,), (1,)), ((), ())), preferred_element_type=F32)


def tn(a, b):
    return lax.dot_general(a, b, (((0,), (0,)), ((), ())), preferred_element_type=F32)


def norm_parts(values):
    centred = values - jnp.mean(values, axis=-1, keepdims=True)
    inverse = lax.rsqrt(jnp.mean(centred * centred, axis=-1, keepdims=True) + EPS)
    return centred * inverse, inverse


def norm_back(grad, normal, inverse, gain):
    scaled = grad * gain
    return inverse * (
        scaled
        - jnp.mean(scaled, axis=-1, keepdims=True)
        - normal * jnp.mean(scaled * normal, axis=-1, keepdims=True)
    )


def three(value):
    high = value.astype(BF).astype(F32)
    rest = value - high
    middle = rest.astype(BF).astype(F32)
    return high, middle, rest - middle


def extra_rows(value, last):
    row = lax.broadcasted_iota(jnp.int32, (16, value.shape[1]), 0)
    high, middle, low = three(value)
    out = jnp.where(row == 0, -high, 0.0)
    out = jnp.where(row == 1, -middle, out)
    out = jnp.where(row == 2, -low, out)
    return jnp.where(row == 3, last, out)


def spread(first, second, route0, route1, experts):
    zero = jnp.zeros_like(first)
    return jnp.concatenate(
        [
            jnp.where(route0 == e, first, jnp.where(route1 == e, second, zero))
            for e in range(experts)
        ],
        axis=0,
    )


def picked(table, route, experts):
    head = table.shape[0] // experts
    out = jnp.zeros((head, table.shape[1]), F32)
    for e in range(experts):
        out = jnp.where(route == e, table[e * head : (e + 1) * head, :], out)
    return out


def key_rows(pair, live, head):
    lane = lax.broadcasted_iota(jnp.int32, pair.shape, 1)
    row = lax.broadcasted_iota(jnp.int32, pair.shape, 0)
    ones = jnp.where(lane < head + 3, 1.0, 0.0)
    mask = jnp.where(row < live, 0.0, MASKED)
    out = jnp.where(lane == head + 3, mask, ones)
    return jnp.where(lane < head, pair.astype(F32), out).astype(BF)


def first_kernel(x, gain, bias, router, proj, routes, normed, pairs, gates):
    experts = router.shape[0] // 2
    normal, _ = norm_parts(x[...].astype(F32))
    out = (normal * gain[...] + bias[...]).astype(BF)
    normed[...] = out
    pairs[...] = nn(out, proj[...]).astype(BF)
    logits = nt(router[...], out)
    route = routes[...]
    chosen = []
    for s in range(2):
        one = jnp.zeros((1, logits.shape[1]), F32)
        for e in range(experts):
            one = jnp.where(route[s : s + 1, :] == e, logits[e : e + 1, :], one)
        chosen.append(one)
    top = jnp.maximum(chosen[0], chosen[1])
    up0, up1 = jnp.exp(chosen[0] - top), jnp.exp(chosen[1] - top)
    inverse = 1.0 / (up0 + up1)
    gates[0:1, :] = up0 * inverse
    gates[1:2, :] = up1 * inverse


def assembled(table, shares, where, experts, start):
    head = table.shape[0] // experts
    share = head // 4
    for o, part in enumerate(shares):
        for e in range(experts):
            at = pl.multiple_of(e * head + where[o] * share, share)
            here = slice(start + e * share, start + (e + 1) * share)
            table[pl.ds(at, share), :] = part[here, :]


def query_kernel(where, normed, t0, t1, t2, t3, routes, queries, q_rows, table, *, experts, scale):
    @pl.when(pl.program_id(0) == 0)
    def _():
        assembled(table, (t0, t1, t2, t3), where, experts, 0)

    every = nt(table[...], normed[...]) * scale
    for s in range(2):
        one = picked(every, routes[s : s + 1, :], experts)
        queries[s] = one.astype(BF)
        q_rows[s] = jnp.concatenate([one, jnp.zeros_like(one)], axis=0).T.astype(BF)


def attend_kernel(live, q, p0, p1, p2, p3, out, kept, keys, values, limit, top, *, head, span):
    part = p0.shape[0]

    @pl.when((pl.program_id(0) == 0) & (pl.program_id(1) == 0))
    def _():
        row = lax.broadcasted_iota(jnp.int32, (LANES, LANES), 0)
        col = lax.broadcasted_iota(jnp.int32, (LANES, LANES), 1)
        move = jnp.where((col == row + head) & (row < head), 1.0, 0.0).astype(BF)
        count = jnp.where(row < head, 1.0, 0.0).astype(BF)
        longest = jnp.zeros((1, LANES), F32)
        for o, p in enumerate((p0, p1, p2, p3)):
            pair = p[...]
            keys[o * part : (o + 1) * part, :] = key_rows(pair, live[o], head)
            turned = nt(move, pair)
            line = lax.broadcasted_iota(jnp.int32, turned.shape, 0)
            values[:, o * part : (o + 1) * part] = jnp.where(line == head, 1.0, turned).astype(BF)
            wide = pair.astype(F32)
            squares = nn((wide * wide).astype(BF), count)
            longest = jnp.maximum(longest, jnp.max(squares, axis=0, keepdims=True))
        limit[...] = jnp.broadcast_to(1.02 * jnp.sqrt(longest), limit.shape)

    query = q[0]
    wide = query.astype(F32)
    length = jnp.sqrt(jnp.sum(wide * wide, axis=0, keepdims=True))
    bound = length * limit[0:1, 0:1]
    top[...] = jnp.zeros_like(top)
    n = query.shape[1]
    rest = jnp.zeros((LANES - head - 16, n), BF)

    @pl.when(jnp.max(bound) > SAFE)
    def _():
        plain = jnp.concatenate(
            [query, extra_rows(jnp.zeros((1, n), F32), 1.0).astype(BF), rest], axis=0
        )

        def peak(j, now):
            at = pl.multiple_of(j * 512, 512)
            scores = nn(keys[pl.ds(at, 512), :], plain)
            return jnp.maximum(now, jnp.max(scores, axis=0, keepdims=True))

        best = lax.fori_loop(0, 4 * part // 512, peak, jnp.full((1, n), -3e38, F32))
        top[...] = jnp.broadcast_to(best, top.shape)

    extended = jnp.concatenate([query, extra_rows(top[0:1, :], 1.0).astype(BF), rest], axis=0)
    total = jnp.zeros((LANES, n), F32)
    for j in range(4 * part // span):
        here = slice(j * span, (j + 1) * span)
        weights = jnp.exp2(nn(keys[here, :], extended)).astype(BF)
        kept[here, :] = weights
        total = total + nn(values[:, here], weights)
    inverse = 1.0 / total[head : head + 1, :]
    out[0, 0:head, :] = total[0:head, :] * inverse
    out[0, head : head + 8, :] = jnp.broadcast_to(inverse, (8, n))


def attend_back_kernel(dot, do, q, *rest, head, places, first):
    if not first:
        before, *rest = rest
    pieces = len(places)
    weights, pairs, after = rest[:pieces], rest[pieces : 2 * pieces], rest[2 * pieces]
    grads = rest[2 * pieces + 1 : 3 * pieces + 1]
    values, turned, both = rest[3 * pieces + 1 :]
    step = pl.program_id(0)
    sizes = [pair.shape[0] for pair in pairs]
    spans = [slice(sum(sizes[:n]), sum(sizes[: n + 1])) for n in range(pieces)]

    @pl.when(step == 0)
    def _():
        row = lax.broadcasted_iota(jnp.int32, (head, LANES), 0)
        col = lax.broadcasted_iota(jnp.int32, (head, LANES), 1)
        same = jnp.where(row == col, 1.0, 0.0).astype(BF)
        for pair, here in zip(pairs, spans):
            rows = pair[...]
            turned[:, here] = nt(same, rows).astype(BF)
            lane = lax.broadcasted_iota(jnp.int32, rows.shape, 1)
            fixed = jnp.where(lane < 3, 1.0, 0.0)
            values[here, :] = jnp.where(lane < head, fixed, rows.astype(F32)).astype(BF)
        both[...] = jnp.zeros_like(both)

    right = jnp.concatenate([q[0], do[0]], axis=0)
    grown = jnp.zeros((head, q.shape[1]), F32)
    for weight, here in zip(weights, spans):
        attention = weight[...]
        scores = (attention.astype(F32) * nn(values[here, :], dot[0])).astype(BF)
        both[here, :] += nn(jnp.concatenate([scores, attention], axis=1), right)
        grown = grown + nn(turned[:, here], scores)
    after[0] = grown if first else before[0] + grown

    @pl.when(step == pl.num_programs(0) - 1)
    def _():
        for grad, here in zip(grads, spans):
            lane = lax.broadcasted_iota(jnp.int32, grad.shape, 1)
            grad[...] = (both[here, :] * jnp.where(lane < head, LN2, 1.0)).astype(BF)


def middle_kernel(
    where, att, routes, gates, x, up, normed,
    f0, f1, f2, f3, rb, gain, bias,
    out, mid_grad, do_rows, do_t, logit, g0, g1, g2, g3,
    we_sum, wr_sum, wo_sum, eb_sum, small, rt_sum, wo,
    *, head, experts,
):
    step = pl.program_id(0)

    @pl.when(step == 0)
    def _():
        for r in (we_sum, wr_sum, wo_sum, eb_sum, small, rt_sum):
            r[...] = jnp.zeros_like(r)
        assembled(wo, (f0, f1, f2, f3), where, experts, f0.shape[0] - experts * (head // 4))

    route0, route1 = routes[0:1, :], routes[1:2, :]
    gate0, gate1 = gates[0:1, :], gates[1:2, :]
    mix0, mix1 = att[0, 0:head, :], att[1, 0:head, :]
    low0, low1 = mix0.astype(BF).astype(F32), mix1.astype(BF).astype(F32)
    mixed = spread(gate0 * low0, gate1 * low1, route0, route1, experts).astype(BF)
    middle = x[...].astype(F32) + tn(mixed, wo[...])
    normal, inverse = norm_parts(middle)
    normed_two = (normal * gain[...] + bias[...]).astype(BF)
    upstream = up[...]
    n2t = normed_two.T
    upt = upstream.T
    ff = f0.shape[1]
    width = middle.shape[1]
    reduced = jnp.zeros(middle.shape, F32)
    two_grad = jnp.zeros(middle.shape, F32)
    for o, f in enumerate((f0, f1, f2, f3)):
        here = slice(o * ff, (o + 1) * ff)
        we, wr = f[0:width, :], f[width : width + ff, :]
        v = nn(normed_two, we) + f[width + ff : width + ff + 16, :].astype(F32)[0:1, :]
        square = v * v
        inner = v * (GELU_A + (GELU_A * GELU_B) * square)
        half = 0.5 + 0.5 * jnp.tanh(inner)
        act = v * half
        slope = half + 2.0 * act * (1.0 - half) * (GELU_A + (3.0 * GELU_A * GELU_B) * square)
        low = act.astype(BF)
        reduced = reduced + nn(low, wr)
        back = nt(upstream, wr) * slope
        back_low = back.astype(BF)
        two_grad = two_grad + nt(back_low, we)
        we_sum[:, here] += nn(n2t, back_low)
        wr_sum[:, here] += nn(upt, low)
        eb_sum[0:1, here] += jnp.sum(back_low.astype(F32), axis=0, keepdims=True)
    out[...] = (middle + reduced + rb[...]).astype(BF)
    wide_up = upstream.astype(F32)
    mid = wide_up + norm_back(two_grad, normal, inverse, gain[...])
    mid_grad[...] = mid
    small[0:1, :] += jnp.sum(wide_up, axis=0, keepdims=True)
    small[1:2, :] += jnp.sum(two_grad * normal, axis=0, keepdims=True)
    small[2:3, :] += jnp.sum(two_grad, axis=0, keepdims=True)
    mid_low = mid.astype(BF)
    wo_sum[...] += nn(mixed, mid_low)
    every = nt(wo[...], mid_low)
    pull0, pull1 = picked(every, route0, experts), picked(every, route1, experts)
    gate_grad0 = jnp.sum(low0 * pull0, axis=0, keepdims=True)
    gate_grad1 = jnp.sum(low1 * pull1, axis=0, keepdims=True)
    both = gate0 * gate_grad0 + gate1 * gate_grad1
    chosen0, chosen1 = gate0 * (gate_grad0 - both), gate1 * (gate_grad1 - both)
    row = lax.broadcasted_iota(jnp.int32, (16, chosen0.shape[1]), 0)
    logit_rows = jnp.where(row == route0, chosen0, jnp.where(row == route1, chosen1, 0.0))
    logit_high = logit_rows.astype(BF)
    logit_low = (logit_rows - logit_high.astype(F32)).astype(BF)
    logit[...] = logit_high
    here_normed = normed[...]
    rt_sum[...] += nn(logit_high, here_normed) + nn(logit_low, here_normed)
    rest = jnp.zeros((LANES - head - 16, row.shape[1]), F32)
    for s, (gate, pull, mix) in enumerate(((gate0, pull0, mix0), (gate1, pull1, mix1))):
        low = (gate * pull * att[s, head : head + 1, :]).astype(BF)
        grad = low.astype(F32)
        delta = jnp.sum(grad * mix, axis=0, keepdims=True)
        do_t[s] = jnp.concatenate([extra_rows(delta, 0.0), rest, grad], axis=0).astype(BF)
        do_rows[s] = jnp.concatenate([jnp.zeros_like(grad), grad], axis=0).T.astype(BF)

    @pl.when(step == pl.num_programs(0) - 1)
    def _():
        share = head // 4
        table = g0.shape[0] - experts * share
        for o, g in enumerate((g0, g1, g2, g3)):
            here = slice(o * ff, (o + 1) * ff)
            g[0:width, :] = we_sum[:, here].astype(BF)
            g[width : 2 * width, :] = wr_sum[:, here].astype(BF)
            line = lax.broadcasted_iota(jnp.int32, (8, ff), 0)
            head_rows = jnp.where(line == 3, eb_sum[0:1, here], small[...])
            g[2 * width : 2 * width + 16, :] = jnp.concatenate(
                [head_rows, rt_sum[0:8, :]], axis=0
            ).astype(BF)
            g[2 * width + 16 : table, :] = jnp.zeros((table - 2 * width - 16, ff), BF)
            for e in range(experts):
                at = pl.multiple_of(e * head + where[o] * share, share)
                g[table + e * share : table + (e + 1) * share, :] = wo_sum[
                    pl.ds(at, share), :
                ].astype(BF)


def last_kernel(
    where, dq, pa, pd, p1, p2, p3, logit, routes, normed, x, mid_grad, gain, wq, proj, router,
    out, s0, s1, s2, s3, wq_sum, sp_sum, small, *, head, experts, scale,
):
    step = pl.program_id(0)

    @pl.when(step == 0)
    def _():
        for r in (wq_sum, sp_sum, small):
            r[...] = jnp.zeros_like(r)

    route0, route1 = routes[0:1, :], routes[1:2, :]
    grad0, grad1 = dq[0] * scale, dq[1] * scale
    placed = spread(grad0, grad1, route0, route1, experts).astype(BF)
    own = jnp.where(step < pl.num_programs(0) // 2, pa[...].astype(F32), pd[...].astype(F32))
    for p in (p1, p2, p3):
        own = own + p[...].astype(F32)
    pair = own.astype(BF)
    normed_grad = tn(placed, wq[...]) + nt(pair, proj[...]) + tn(logit[...], router[...])
    here_normed = normed[...]
    wq_sum[...] += nn(placed, here_normed)
    sp_sum[...] += tn(pair, here_normed)
    normal, inverse = norm_parts(x[...].astype(F32))
    out[...] = mid_grad[...] + norm_back(normed_grad, normal, inverse, gain[...])
    small[0:1, :] += jnp.sum(normed_grad * normal, axis=0, keepdims=True)
    small[1:2, :] += jnp.sum(normed_grad, axis=0, keepdims=True)

    @pl.when(step == pl.num_programs(0) - 1)
    def _():
        share = head // 4
        block = sp_sum.shape[1] // 4
        each = sp_sum.shape[0] // 4
        table = experts * share
        for o, s in enumerate((s0, s1, s2, s3)):
            owner = where[o]
            for e in range(experts):
                at = pl.multiple_of(e * head + owner * share, share)
                s[e * share : (e + 1) * share, :] = wq_sum[pl.ds(at, share), :].astype(BF)
            lanes = pl.ds(pl.multiple_of(owner * block, block), block)
            s[table + each : table + each + 16, :] = jnp.zeros((16, 4 * block), BF)
            ends = jnp.concatenate([small[:, lanes], jnp.zeros((8, block), F32)], axis=0)
            s[table + each : table + each + 16, 0:block] = ends.astype(BF)
            for g in range(4):
                piece = sp_sum[g * each : (g + 1) * each, lanes]
                s[table : table + each, g * block : (g + 1) * block] = piece.astype(BF)


def swapped(value, bit):
    return lax.ppermute(value, "mp", [(i, i ^ bit) for i in range(4)])


def four(value):
    across = swapped(value, 2)
    return value, swapped(value, 1), across, swapped(across, 1)


def summed(a, b):
    return (a.astype(F32) + b.astype(F32)).astype(BF)


def group_sum(parts):
    far = summed(parts[2], swapped(parts[3], 1))
    near = summed(parts[0], swapped(parts[1], 1))
    return near, swapped(far, 2)


def sent_to_all(value, axes):
    n = lax.axis_size(axes)
    wide = jnp.broadcast_to(value[None], (n,) + value.shape)
    return lax.all_to_all(wide, axes, split_axis=0, concat_axis=0, tiled=True)


def spec(shape, index):
    return pl.BlockSpec(shape, index)


def fixed(shape):
    return pl.BlockSpec(shape, lambda *_: (0,) * len(shape))


def shape(dims, kind):
    return jax.ShapeDtypeStruct(dims, kind)


SMEM = pl.BlockSpec(memory_space=pltpu.SMEM)
PARAMS = pltpu.CompilerParams(vmem_limit_bytes=58 * 2**20)


def cost(us):
    return pl.CostEstimate(flops=int(us * 1.1e9), bytes_accessed=1024, transcendentals=0)


def tied(value, *others):
    return lax.optimization_barrier((value, *others))[0]


def on_device(
    block_input, routes, lengths, first_gain, first_bias, router_weight, shared_proj,
    query_weight, output_weight, second_gain, second_bias, expand_weight, expand_bias,
    reduce_weight, reduce_bias, upstream_grad,
):
    tokens, width = block_input.shape[1], block_input.shape[2]
    experts = router_weight.shape[1]
    head = query_weight.shape[0] * lax.axis_size("mp")
    dp = lax.axis_size("dp")
    units = expand_weight.shape[1]
    me = lax.axis_index("mp")
    owners = me ^ jnp.arange(4, dtype=jnp.int32)
    live = jnp.clip(lengths[0] - owners * tokens, 0, tokens)
    x = block_input.reshape(tokens, width)
    up = upstream_grad.reshape(tokens, width)
    routes_t = routes.reshape(tokens, 2).T
    router_t = jnp.concatenate([router_weight.T, jnp.zeros((experts, width), BF)], axis=0)
    gain1, bias1 = first_gain[None], first_bias[None]
    gain2, bias2 = second_gain[None], second_bias[None]

    tb = 512
    rows = spec((tb, width), lambda i: (i, 0))
    cols2 = spec((2, tb), lambda i: (0, i))
    normed, pairs, gates = pl.pallas_call(
        first_kernel,
        grid=(tokens // tb,),
        in_specs=[rows, fixed((1, width)), fixed((1, width)), fixed((2 * experts, width)),
                  fixed((width, 2 * head)), cols2],
        out_specs=[rows, spec((tb, 2 * head), lambda i: (i, 0)), cols2],
        out_shape=[shape((tokens, width), BF), shape((tokens, 2 * head), BF), shape((2, tokens), F32)],
        compiler_params=PARAMS,
        cost_estimate=cost(5),
    )(x, gain1, bias1, router_t, shared_proj, routes_t)

    pair_across = swapped(pairs, 2)
    pair_beside = swapped(pairs, 1)
    both = jnp.concatenate([query_weight, output_weight], axis=0)
    shares = sent_to_all(both, "dp")
    shares = shares.reshape(experts, dp // experts, 2, head // 4, -1).transpose(2, 0, 3, 1, 4)
    shares = shares.reshape(2, experts * head // 4, width)
    table = [shares[0]] + [swapped(shares[0], bit) for bit in (1, 2, 3)]
    feed = jnp.concatenate(
        [expand_weight, reduce_weight, jnp.broadcast_to(expand_bias[None], (16, units)), shares[1]],
        axis=0,
    )
    feed, pair_across = lax.optimization_barrier((feed, pair_across))
    pair = (pairs, pair_beside, pair_across, swapped(pair_across, 1))
    feed_across = swapped(feed, 2)
    queries, q_rows, wq = pl.pallas_call(
        functools.partial(query_kernel, experts=experts, scale=0.125 * LOG2E),
        grid=(tokens // tb,),
        in_specs=[SMEM, rows] + [fixed((experts * head // 4, width))] * 4 + [cols2],
        out_specs=[spec((2, head, tb), lambda i: (0, 0, i)), spec((2, tb, LANES), lambda i: (0, i, 0)),
                   fixed((experts * head, width))],
        out_shape=[shape((2, head, tokens), BF), shape((2, tokens, LANES), BF),
                   shape((experts * head, width), BF)],
        compiler_params=PARAMS,
        cost_estimate=cost(5),
    )(owners, normed, *table, routes_t)

    tq = 512
    att, kept = pl.pallas_call(
        functools.partial(attend_kernel, head=head, span=4 * tokens),
        grid=(2, tokens // tq),
        in_specs=[SMEM, spec((1, head, tq), lambda s, i: (s, 0, i))] + [fixed((tokens, 2 * head))] * 4,
        out_specs=[spec((1, head + 8, tq), lambda s, i: (s, 0, i)),
                   spec((4 * tokens, tq), lambda s, i: (0, s * (tokens // tq) + i))],
        out_shape=[shape((2, head + 8, tokens), F32), shape((4 * tokens, 2 * tokens), BF)],
        scratch_shapes=[
            pltpu.VMEM((4 * tokens, LANES), BF), pltpu.VMEM((LANES, 4 * tokens), BF),
            pltpu.VMEM((8, LANES), F32), pltpu.VMEM((8, tq), F32),
        ],
        compiler_params=PARAMS,
        cost_estimate=cost(33),
    )(live, queries, *pair)

    feed_across = tied(feed_across, att)
    feeds = (feed, swapped(feed, 1), feed_across, swapped(feed_across, 1))

    tm = 512
    rows = spec((tm, width), lambda i: (i, 0))
    cols2 = spec((2, tm), lambda i: (0, i))
    tail = 2 * width + 64
    share = experts * head // 4
    slot = tail + share
    both_rows = spec((2, tm, LANES), lambda i: (0, i, 0))
    both_cols = spec((2, LANES, tm), lambda i: (0, 0, i))
    att_cols = spec((2, head + 8, tm), lambda i: (0, 0, i))
    block_out, mid_grad, do_rows, do_t, logit, *ffn = pl.pallas_call(
        functools.partial(middle_kernel, head=head, experts=experts),
        grid=(tokens // tm,),
        in_specs=[SMEM, att_cols, cols2, cols2, rows, rows, rows]
        + [fixed(feed.shape)] * 4 + [fixed((1, width))] * 3,
        out_specs=[rows, rows, both_rows, both_cols, spec((16, tm), lambda i: (0, i))]
        + [fixed((slot, units))] * 4,
        out_shape=[shape((tokens, width), BF), shape((tokens, width), F32), shape((2, tokens, LANES), BF),
                   shape((2, LANES, tokens), BF), shape((16, tokens), BF)]
        + [shape((slot, units), BF)] * 4,
        scratch_shapes=[
            pltpu.VMEM((width, 4 * units), F32), pltpu.VMEM((width, 4 * units), F32),
            pltpu.VMEM((experts * head, width), F32), pltpu.VMEM((8, 4 * units), F32),
            pltpu.VMEM((8, width), F32), pltpu.VMEM((16, width), F32),
            pltpu.VMEM((experts * head, width), BF),
        ],
        compiler_params=PARAMS,
        cost_estimate=cost(50),
    )(owners, att, routes_t, gates, x, up, normed, *feeds, reduce_bias[None].astype(F32),
      gain2, bias2)

    def back_call(places, before, us):
        many = sum(size for _, _, size in places)
        first = before is None
        tq = 512
        per = tokens // tq
        row_block = spec((1, tq, LANES), lambda i: (i // per, i % per, 0))
        col_block = spec((1, LANES, tq), lambda i: (i // per, 0, i % per))
        grad_block = spec((1, head, tq), lambda i: (i // per, 0, i % per))
        return pl.pallas_call(
            functools.partial(attend_back_kernel, head=head, places=places, first=first),
            grid=(2 * per,),
            in_specs=[col_block, row_block, row_block] + [grad_block] * (not first)
            + [spec((size, tq), lambda i, at=o * tokens // size + at: (at, i)) for o, at, size in places]
            + [spec((size, 2 * head), lambda i, at=at: (at, 0)) for _, at, size in places],
            out_specs=[grad_block] + [fixed((size, 2 * head)) for _, _, size in places],
            out_shape=[shape((2, head, tokens), F32)]
            + [shape((size, 2 * head), BF) for _, _, size in places],
            input_output_aliases={} if first else {3: 0},
            scratch_shapes=[
                pltpu.VMEM((many, LANES), BF), pltpu.VMEM((head, many), BF),
                pltpu.VMEM((many, LANES), F32),
            ],
            compiler_params=PARAMS,
            cost_estimate=cost(us),
        )(do_t, do_rows, q_rows, *([] if first else [before]), *[kept] * len(places),
          *[pair[o] for o, _, _ in places])

    def by_holder(rows_of):
        each = rows_of.reshape(experts, head // 4, dp // experts, -1).transpose(0, 2, 1, 3)
        return each.reshape(dp, -1, width)

    half = tokens // 2
    arrived = [swapped(ffn[bit], bit) for bit in (3, 2, 1)]
    q_grad, key3, key2, key0a = back_call(
        [(3, 0, tokens), (2, 0, tokens), (0, 0, half)], None, 55
    )
    own = sum([a.astype(F32) for a in arrived], ffn[0].astype(F32)).astype(BF)
    own = jnp.concatenate([own[:tail].reshape(dp, -1, width), by_holder(own[tail:])], axis=1)
    q_grad, own, key3, key2 = lax.optimization_barrier((q_grad, own, key3, key2))
    key_from3, key_from2 = swapped(key3, 3), swapped(key2, 2)
    arrived = lax.all_to_all(own, "dp", split_axis=0, concat_axis=0, tiled=True)
    q_grad, key1, key0b = back_call([(1, 0, tokens), (0, 1, half)], q_grad, 35)
    piece = jnp.sum(arrived.astype(F32), axis=0)
    q_grad, piece, key1 = lax.optimization_barrier((q_grad, piece, key1))
    key_from1 = swapped(key1, 1)
    total = sent_to_all(piece[: tail // dp].astype(BF), "dp").reshape(tail, units)
    wo_total = piece[tail // dp :].reshape(head // 4, -1)

    tl = 512
    rows = spec((tl, width), lambda i: (i, 0))
    cols2 = spec((2, tl), lambda i: (0, i))
    pair_rows = spec((tl, 2 * head), lambda i: (i, 0))
    count = half // tl
    first_rows = spec((tl, 2 * head), lambda i: (jnp.minimum(i, count - 1), 0))
    second_rows = spec((tl, 2 * head), lambda i: (jnp.maximum(i - count, 0), 0))
    input_grad, *last = pl.pallas_call(
        functools.partial(last_kernel, head=head, experts=experts, scale=0.125),
        grid=(tokens // tl,),
        in_specs=[SMEM, spec((2, head, tl), lambda i: (0, 0, i)), first_rows, second_rows, pair_rows, pair_rows,
                  pair_rows,
                  spec((16, tl), lambda i: (0, i)), cols2, rows, rows, rows, fixed((1, width)),
                  fixed((experts * head, width)), fixed((width, 2 * head)), fixed((2 * experts, width))],
        out_specs=[rows] + [fixed((share + 48, width))] * 4,
        out_shape=[shape((tokens, width), F32)] + [shape((share + 48, width), BF)] * 4,
        scratch_shapes=[
            pltpu.VMEM((experts * head, width), F32), pltpu.VMEM((2 * head, width), F32),
            pltpu.VMEM((8, width), F32),
        ],
        compiler_params=PARAMS,
        cost_estimate=cost(10),
    )(owners, q_grad, key0a, key0b, key_from1, key_from2, key_from3, logit, routes_t, normed, x, mid_grad, gain1, wq,
      shared_proj, router_t)

    near, far = group_sum(last)
    mine, total = lax.optimization_barrier((summed(near, far), total))
    total = total.astype(F32)
    ends = jnp.broadcast_to(mine[share:][None], (dp, 48, width))
    each = jnp.concatenate([by_holder(mine[:share]), ends], axis=1)
    got = lax.all_to_all(each, "dp", split_axis=0, concat_axis=0, tiled=True)
    got = jnp.sum(got.astype(F32), axis=0)
    wq_total = got[: share // dp].reshape(head // 4, -1)
    ends = got[share // dp :]
    block = width // 4
    each = 2 * head // 4
    shared_total = jnp.concatenate(
        [ends[:each, g * block : (g + 1) * block] for g in range(4)], axis=0
    )
    cut = lax.dynamic_slice_in_dim(total[2 * width : 2 * width + 16], me * block, block, axis=1)
    return (
        block_out.reshape(1, tokens, width),
        input_grad.reshape(1, tokens, width),
        ends[each, :block],
        ends[each + 1, :block],
        cut[8 : 8 + experts].T,
        shared_total.T,
        wq_total,
        wo_total,
        cut[1],
        cut[2],
        total[:width],
        total[2 * width + 3],
        total[width : 2 * width].T,
        cut[0],
    )


def solution(mesh):
    both = P("dp", "mp", None)
    table = P("mp", "dp")
    placed = (
        both, both, P("dp"), P(), P(), P(), P(), table, table, P(), P(), P(None, "mp"), P("mp"),
        P("mp", None), P(), both,
    )
    given = (
        both, both, P("mp"), P("mp"), P("mp", None), P("mp", None), table, table, P("mp"), P("mp"),
        P(None, "mp"), P("mp"), P("mp", None), P("mp"),
    )
    return jax.shard_map(on_device, mesh=mesh, in_specs=placed, out_specs=given, check_vma=False)
```

```python
import functools

import jax
import jax.numpy as jnp
from jax import lax
from jax.experimental import pallas as pl
from jax.experimental.pallas import tpu as pltpu
from jax.sharding import PartitionSpec as P

F32 = jnp.float32
BF = jnp.bfloat16
EPS = 1e-05
LOG2E = 1.4426950408889634
LN2 = 0.6931471805599453
MASKED = -1e30
GELU_A = 0.7978845608028654
GELU_B = 0.044715
SAFE = 60.0
LANES = 128


def nn(a, b):
    return lax.dot_general(a, b, (((1,), (0,)), ((), ())), preferred_element_type=F32)


def nt(a, b):
    return lax.dot_general(a, b, (((1,), (1,)), ((), ())), preferred_element_type=F32)


def tn(a, b):
    return lax.dot_general(a, b, (((0,), (0,)), ((), ())), preferred_element_type=F32)


def norm_parts(values):
    centred = values - jnp.mean(values, axis=-1, keepdims=True)
    inverse = lax.rsqrt(jnp.mean(centred * centred, axis=-1, keepdims=True) + EPS)
    return centred * inverse, inverse


def norm_back(grad, normal, inverse, gain):
    scaled = grad * gain
    return inverse * (
        scaled
        - jnp.mean(scaled, axis=-1, keepdims=True)
        - normal * jnp.mean(scaled * normal, axis=-1, keepdims=True)
    )


def three(value):
    high = value.astype(BF).astype(F32)
    rest = value - high
    middle = rest.astype(BF).astype(F32)
    return high, middle, rest - middle


def extra_rows(value, last):
    row = lax.broadcasted_iota(jnp.int32, (16, value.shape[1]), 0)
    high, middle, low = three(value)
    out = jnp.where(row == 0, -high, 0.0)
    out = jnp.where(row == 1, -middle, out)
    out = jnp.where(row == 2, -low, out)
    return jnp.where(row == 3, last, out)


def spread(first, second, route0, route1, experts):
    zero = jnp.zeros_like(first)
    return jnp.concatenate(
        [
            jnp.where(route0 == e, first, jnp.where(route1 == e, second, zero))
            for e in range(experts)
        ],
        axis=0,
    )


def picked(table, route, experts):
    head = table.shape[0] // experts
    out = jnp.zeros((head, table.shape[1]), F32)
    for e in range(experts):
        out = jnp.where(route == e, table[e * head : (e + 1) * head, :], out)
    return out


def key_rows(pair, live, head):
    lane = lax.broadcasted_iota(jnp.int32, pair.shape, 1)
    row = lax.broadcasted_iota(jnp.int32, pair.shape, 0)
    ones = jnp.where(lane < head + 3, 1.0, 0.0)
    mask = jnp.where(row < live, 0.0, MASKED)
    out = jnp.where(lane == head + 3, mask, ones)
    return jnp.where(lane < head, pair.astype(F32), out).astype(BF)


def first_kernel(x, gain, bias, router, proj, routes, normed, pairs, gates):
    experts = router.shape[0] // 2
    normal, _ = norm_parts(x[...].astype(F32))
    out = (normal * gain[...] + bias[...]).astype(BF)
    normed[...] = out
    pairs[...] = nn(out, proj[...]).astype(BF)
    logits = nt(router[...], out)
    route = routes[...]
    chosen = []
    for s in range(2):
        one = jnp.zeros((1, logits.shape[1]), F32)
        for e in range(experts):
            one = jnp.where(route[s : s + 1, :] == e, logits[e : e + 1, :], one)
        chosen.append(one)
    top = jnp.maximum(chosen[0], chosen[1])
    up0, up1 = jnp.exp(chosen[0] - top), jnp.exp(chosen[1] - top)
    inverse = 1.0 / (up0 + up1)
    gates[0:1, :] = up0 * inverse
    gates[1:2, :] = up1 * inverse


def query_kernel(normed, table, routes, queries, q_rows, *, experts, scale):
    every = nt(table[...], normed[...]) * scale
    for s in range(2):
        one = picked(every, routes[s : s + 1, :], experts)
        queries[s] = one.astype(BF)
        q_rows[s] = jnp.concatenate([one, jnp.zeros_like(one)], axis=0).T.astype(BF)


def assembled(table, shares, where, experts, start):
    head = table.shape[0] // experts
    share = head // 4
    for o, part in enumerate(shares):
        for e in range(experts):
            at = pl.multiple_of(e * head + where[o] * share, share)
            here = slice(start + e * share, start + (e + 1) * share)
            table[pl.ds(at, share), :] = part[here, :]


def attend_kernel(where, length, q, p0, p1, p2, p3, out, kept, keys, values, limit, top, *, head, span):
    part = p0.shape[0]

    @pl.when((pl.program_id(0) == 0) & (pl.program_id(1) == 0))
    def _():
        row = lax.broadcasted_iota(jnp.int32, (LANES, LANES), 0)
        col = lax.broadcasted_iota(jnp.int32, (LANES, LANES), 1)
        move = jnp.where((col == row + head) & (row < head), 1.0, 0.0).astype(BF)
        count = jnp.where(row < head, 1.0, 0.0).astype(BF)
        longest = jnp.zeros((1, LANES), F32)
        for o, p in enumerate((p0, p1, p2, p3)):
            pair = p[...]
            live = length[0] - where[o] * part
            keys[o * part : (o + 1) * part, :] = key_rows(pair, live, head)
            turned = nt(move, pair)
            line = lax.broadcasted_iota(jnp.int32, turned.shape, 0)
            values[:, o * part : (o + 1) * part] = jnp.where(line == head, 1.0, turned).astype(BF)
            wide = pair.astype(F32)
            squares = nn((wide * wide).astype(BF), count)
            longest = jnp.maximum(longest, jnp.max(squares, axis=0, keepdims=True))
        limit[...] = jnp.broadcast_to(1.02 * jnp.sqrt(longest), limit.shape)

    query = q[0]
    wide = query.astype(F32)
    length = jnp.sqrt(jnp.sum(wide * wide, axis=0, keepdims=True))
    bound = length * limit[0:1, 0:1]
    top[...] = jnp.zeros_like(top)
    n = query.shape[1]
    rest = jnp.zeros((LANES - head - 16, n), BF)

    @pl.when(jnp.max(bound) > SAFE)
    def _():
        plain = jnp.concatenate(
            [query, extra_rows(jnp.zeros((1, n), F32), 1.0).astype(BF), rest], axis=0
        )

        def peak(j, now):
            at = pl.multiple_of(j * 512, 512)
            scores = nn(keys[pl.ds(at, 512), :], plain)
            return jnp.maximum(now, jnp.max(scores, axis=0, keepdims=True))

        best = lax.fori_loop(0, 4 * part // 512, peak, jnp.full((1, n), -3e38, F32))
        top[...] = jnp.broadcast_to(best, top.shape)

    extended = jnp.concatenate([query, extra_rows(top[0:1, :], 1.0).astype(BF), rest], axis=0)
    total = jnp.zeros((LANES, n), F32)
    for j in range(4 * part // span):
        here = slice(j * span, (j + 1) * span)
        weights = jnp.exp2(nn(keys[here, :], extended)).astype(BF)
        kept[here, :] = weights
        total = total + nn(values[:, here], weights)
    inverse = 1.0 / total[head : head + 1, :]
    out[0, 0:head, :] = total[0:head, :] * inverse
    out[0, head : head + 8, :] = jnp.broadcast_to(inverse, (8, n))


def attend_back_kernel(dot, do, q, *rest, head, places, first, carry):
    if not first:
        before, *rest = rest
    if carry:
        carried, *rest = rest
    pieces = len(places)
    weights, pairs, after = rest[:pieces], rest[pieces : 2 * pieces], rest[2 * pieces]
    grads = rest[2 * pieces + 1 : 3 * pieces + 1]
    values, turned, both = rest[3 * pieces + 1 :]
    step = pl.program_id(0)
    sizes = [pair.shape[0] for pair in pairs]
    spans = [slice(sum(sizes[:n]), sum(sizes[: n + 1])) for n in range(pieces)]

    @pl.when(step == 0)
    def _():
        row = lax.broadcasted_iota(jnp.int32, (head, LANES), 0)
        col = lax.broadcasted_iota(jnp.int32, (head, LANES), 1)
        same = jnp.where(row == col, 1.0, 0.0).astype(BF)
        for pair, here in zip(pairs, spans):
            rows = pair[...]
            turned[:, here] = nt(same, rows).astype(BF)
            lane = lax.broadcasted_iota(jnp.int32, rows.shape, 1)
            fixed = jnp.where(lane < 3, 1.0, 0.0)
            values[here, :] = jnp.where(lane < head, fixed, rows.astype(F32)).astype(BF)
        both[...] = jnp.zeros_like(both)

    right = jnp.concatenate([q[0], do[0]], axis=0)
    grown = jnp.zeros((head, q.shape[1]), F32)
    for weight, here in zip(weights, spans):
        attention = weight[...]
        scores = (attention.astype(F32) * nn(values[here, :], dot[0])).astype(BF)
        both[here, :] += nn(jnp.concatenate([scores, attention], axis=1), right)
        grown = grown + nn(turned[:, here], scores)
    after[0] = grown if first else before[0] + grown

    @pl.when(step == pl.num_programs(0) - 1)
    def _():
        for n, (grad, here) in enumerate(zip(grads, spans)):
            at = 0
            if carry and n == 0:
                at = carried.shape[0]
                grad[0:at, :] = carried[...]
            size = sizes[n]
            lane = lax.broadcasted_iota(jnp.int32, (size, LANES), 1)
            grad[at : at + size, :] = (both[here, :] * jnp.where(lane < head, LN2, 1.0)).astype(BF)


def middle_kernel(
    where, att, routes, gates, x, up, normed,
    f0, f1, f2, f3, gain, bias,
    active, kept, mid_grad, do_rows, do_t, logit, g0, g1, g2, g3,
    we_sum, wr_sum, wo_sum, eb_sum, small, rt_sum, wo,
    *, head, experts,
):
    step = pl.program_id(0)

    @pl.when(step == 0)
    def _():
        for r in (we_sum, wr_sum, wo_sum, eb_sum, small, rt_sum):
            r[...] = jnp.zeros_like(r)
        assembled(wo, (f0, f1, f2, f3), where, experts, f0.shape[0] - experts * (head // 4))

    route0, route1 = routes[0:1, :], routes[1:2, :]
    gate0, gate1 = gates[0:1, :], gates[1:2, :]
    mix0, mix1 = att[0, 0:head, :], att[1, 0:head, :]
    low0, low1 = mix0.astype(BF).astype(F32), mix1.astype(BF).astype(F32)
    mixed = spread(gate0 * low0, gate1 * low1, route0, route1, experts).astype(BF)
    middle = x[...].astype(F32) + tn(mixed, wo[...])
    normal, inverse = norm_parts(middle)
    normed_two = (normal * gain[...] + bias[...]).astype(BF)
    upstream = up[...]
    n2t = normed_two.T
    upt = upstream.T
    ff = f0.shape[1]
    width = middle.shape[1]
    two_grad = jnp.zeros(middle.shape, F32)
    backs = []
    for o, f in enumerate((f0, f1, f2, f3)):
        here = slice(o * ff, (o + 1) * ff)
        v = nn(normed_two, f[0:width, :])
        v = v + f[width + ff : width + ff + 16, :].astype(F32)[0:1, :]
        square = v * v
        inner = v * (GELU_A + (GELU_A * GELU_B) * square)
        half = 0.5 + 0.5 * jnp.tanh(inner)
        act = v * half
        slope = half + act * (1.0 - half) * (2.0 * GELU_A + (6.0 * GELU_A * GELU_B) * square)
        active[:, here] = act.astype(BF)
        backs.append((nt(upstream, f[width : width + ff, :]) * slope).astype(BF))
    for o, f in enumerate((f0, f1, f2, f3)):
        here = slice(o * ff, (o + 1) * ff)
        back = backs[o]
        two_grad = two_grad + nt(back, f[0:width, :])
        we_sum[:, here] += nn(n2t, back)
        wr_sum[:, here] += nn(upt, active[:, here])
        eb_sum[0:1, here] += jnp.sum(back.astype(F32), axis=0, keepdims=True)
    kept[...] = middle.astype(BF)
    wide_up = upstream.astype(F32)
    mid = wide_up + norm_back(two_grad, normal, inverse, gain[...])
    mid_grad[...] = mid.astype(BF)
    small[0:1, :] += jnp.sum(wide_up, axis=0, keepdims=True)
    small[1:2, :] += jnp.sum(two_grad * normal, axis=0, keepdims=True)
    small[2:3, :] += jnp.sum(two_grad, axis=0, keepdims=True)
    mid_low = mid.astype(BF)
    wo_sum[...] += nn(mixed, mid_low)
    every = nt(wo[...], mid_low)
    pull0, pull1 = picked(every, route0, experts), picked(every, route1, experts)
    gate_grad0 = jnp.sum(low0 * pull0, axis=0, keepdims=True)
    gate_grad1 = jnp.sum(low1 * pull1, axis=0, keepdims=True)
    both = gate0 * gate_grad0 + gate1 * gate_grad1
    chosen0, chosen1 = gate0 * (gate_grad0 - both), gate1 * (gate_grad1 - both)
    row = lax.broadcasted_iota(jnp.int32, (16, chosen0.shape[1]), 0)
    logit_rows = jnp.where(row == route0, chosen0, jnp.where(row == route1, chosen1, 0.0))
    logit_high = logit_rows.astype(BF)
    logit_low = (logit_rows - logit_high.astype(F32)).astype(BF)
    logit[...] = logit_high
    here_normed = normed[...]
    rt_sum[...] += nn(logit_high, here_normed) + nn(logit_low, here_normed)
    rest = jnp.zeros((LANES - head - 16, row.shape[1]), F32)
    for s, (gate, pull, mix) in enumerate(((gate0, pull0, mix0), (gate1, pull1, mix1))):
        low = (gate * pull * att[s, head : head + 1, :]).astype(BF)
        grad = low.astype(F32)
        delta = jnp.sum(grad * mix, axis=0, keepdims=True)
        do_t[s] = jnp.concatenate([extra_rows(delta, 0.0), rest, grad], axis=0).astype(BF)
        do_rows[s] = jnp.concatenate([jnp.zeros_like(grad), grad], axis=0).T.astype(BF)

    @pl.when(step == pl.num_programs(0) - 1)
    def _():
        share = head // 4
        table = g0.shape[0] - experts * share
        for o, g in enumerate((g0, g1, g2, g3)):
            here = slice(o * ff, (o + 1) * ff)
            g[0:width, :] = we_sum[:, here].astype(BF)
            g[width : 2 * width, :] = wr_sum[:, here].astype(BF)
            line = lax.broadcasted_iota(jnp.int32, (8, ff), 0)
            head_rows = jnp.where(line == 3, eb_sum[0:1, here], small[...])
            g[2 * width : 2 * width + 16, :] = jnp.concatenate(
                [head_rows, rt_sum[0:8, :]], axis=0
            ).astype(BF)
            g[2 * width + 16 : table, :] = jnp.zeros((table - 2 * width - 16, ff), BF)
            for e in range(experts):
                at = pl.multiple_of(e * head + where[o] * share, share)
                g[table + e * share : table + (e + 1) * share, :] = wo_sum[
                    pl.ds(at, share), :
                ].astype(BF)


def last_kernel(
    where, dq, p0, p1, p2, p3, logit, routes, normed, x, wq, proj, router,
    out, s0, s1, s2, s3, wq_sum, sp_sum, small, *, head, experts, scale,
):
    step = pl.program_id(0)

    @pl.when(step == 0)
    def _():
        for r in (wq_sum, sp_sum, small):
            r[...] = jnp.zeros_like(r)

    route0, route1 = routes[0:1, :], routes[1:2, :]
    grad0, grad1 = dq[0] * scale, dq[1] * scale
    placed = spread(grad0, grad1, route0, route1, experts).astype(BF)
    own = p0[...].astype(F32)
    for p in (p1, p2, p3):
        own = own + p[...].astype(F32)
    pair = own.astype(BF)
    normed_grad = tn(placed, wq[...]) + nt(pair, proj[...]) + tn(logit[...], router[...])
    here_normed = normed[...]
    wq_sum[...] += nn(placed, here_normed)
    sp_sum[...] += tn(pair, here_normed)
    normal, _ = norm_parts(x[...].astype(F32))
    out[...] = normed_grad.astype(BF)
    small[0:1, :] += jnp.sum(normed_grad * normal, axis=0, keepdims=True)
    small[1:2, :] += jnp.sum(normed_grad, axis=0, keepdims=True)

    @pl.when(step == pl.num_programs(0) - 1)
    def _():
        share = head // 4
        block = sp_sum.shape[1] // 4
        each = sp_sum.shape[0] // 4
        table = experts * share
        for o, s in enumerate((s0, s1, s2, s3)):
            owner = where[o]
            for e in range(experts):
                at = pl.multiple_of(e * head + owner * share, share)
                s[e * share : (e + 1) * share, :] = wq_sum[pl.ds(at, share), :].astype(BF)
            lanes = pl.ds(pl.multiple_of(owner * block, block), block)
            s[table + each : table + each + 16, :] = jnp.zeros((16, 4 * block), BF)
            line = lax.broadcasted_iota(jnp.int32, (16, block), 0)
            for g in range(2):
                ends = jnp.where(line == 0, small[g : g + 1, lanes], 0.0)
                s[table + each : table + each + 16, g * block : (g + 1) * block] = ends.astype(BF)
            for g in range(4):
                piece = sp_sum[g * each : (g + 1) * each, lanes]
                s[table : table + each, g * block : (g + 1) * block] = piece.astype(BF)


def outputs_kernel(active, middle, r0, r1, r2, r3, rb, normed_grad, x, mid_grad, gain, out, x_grad):
    ff = r0.shape[0]
    total = middle[...].astype(F32) + rb[...]
    for o, r in enumerate((r0, r1, r2, r3)):
        total = total + nn(active[:, o * ff : (o + 1) * ff], r[...])
    out[...] = total.astype(BF)
    normal, inverse = norm_parts(x[...].astype(F32))
    back = norm_back(normed_grad[...].astype(F32), normal, inverse, gain[...])
    x_grad[...] = mid_grad[...].astype(F32) + back


def swapped(value, bit):
    return lax.ppermute(value, "mp", [(i, i ^ bit) for i in range(4)])


def four(value):
    across = swapped(value, 2)
    return value, swapped(value, 1), across, swapped(across, 1)


def summed(a, b):
    return (a.astype(F32) + b.astype(F32)).astype(BF)


def sent_to_all(value, axes):
    n = lax.axis_size(axes)
    wide = jnp.broadcast_to(value[None], (n,) + value.shape)
    return lax.all_to_all(wide, axes, split_axis=0, concat_axis=0, tiled=True)


def whole_table(share, experts):
    dp, mp = lax.axis_size("dp"), lax.axis_size("mp")
    rows, cols = share.shape
    every = sent_to_all(share, ("dp", "mp"))
    each = every.reshape(experts, dp // experts, mp, rows, cols)
    return each.transpose(0, 2, 3, 1, 4).reshape(experts * mp * rows, dp // experts * cols)


def spec(shape, index):
    return pl.BlockSpec(shape, index)


def fixed(shape):
    return pl.BlockSpec(shape, lambda *_: (0,) * len(shape))


def shape(dims, kind):
    return jax.ShapeDtypeStruct(dims, kind)


SMEM = pl.BlockSpec(memory_space=pltpu.SMEM)
PARAMS = pltpu.CompilerParams(vmem_limit_bytes=58 * 2**20)


def cost(us):
    return pl.CostEstimate(flops=int(us * 1.1e9), bytes_accessed=1024, transcendentals=0)


def tied(value, *others):
    return lax.optimization_barrier((value, *others))[0]


def on_device(
    block_input, routes, lengths, first_gain, first_bias, router_weight, shared_proj,
    query_weight, output_weight, second_gain, second_bias, expand_weight, expand_bias,
    reduce_weight, reduce_bias, upstream_grad,
):
    tokens, width = block_input.shape[1], block_input.shape[2]
    experts = router_weight.shape[1]
    head = query_weight.shape[0] * lax.axis_size("mp")
    dp = lax.axis_size("dp")
    units = expand_weight.shape[1]
    me = lax.axis_index("mp")
    owners = me ^ jnp.arange(4, dtype=jnp.int32)
    x = block_input.reshape(tokens, width)
    up = upstream_grad.reshape(tokens, width)
    routes_t = routes.reshape(tokens, 2).T
    router_t = jnp.pad(router_weight.T, ((0, experts), (0, 0)))
    gain1, bias1 = first_gain[None], first_bias[None]
    gain2, bias2 = second_gain[None], second_bias[None]

    wq = whole_table(query_weight, experts)

    tb = 512
    rows = spec((tb, width), lambda i: (i, 0))
    cols2 = spec((2, tb), lambda i: (0, i))
    normed, pairs, gates = pl.pallas_call(
        first_kernel,
        grid=(tokens // tb,),
        in_specs=[rows, fixed((1, width)), fixed((1, width)), fixed((2 * experts, width)),
                  fixed((width, 2 * head)), cols2],
        out_specs=[rows, spec((tb, 2 * head), lambda i: (i, 0)), cols2],
        out_shape=[shape((tokens, width), BF), shape((tokens, 2 * head), BF), shape((2, tokens), F32)],
        compiler_params=PARAMS,
        cost_estimate=cost(5),
    )(x, gain1, bias1, router_t, shared_proj, routes_t)

    pair_across = swapped(pairs, 2)
    pair_beside = swapped(pairs, 1)
    output_weight, wq = lax.optimization_barrier((output_weight, wq))
    o_share = sent_to_all(output_weight, "dp")
    o_share = o_share.reshape(experts, dp // experts, head // 4, -1).transpose(0, 2, 1, 3)
    o_share = o_share.reshape(experts * head // 4, width)
    queries, q_rows = pl.pallas_call(
        functools.partial(query_kernel, experts=experts, scale=0.125 * LOG2E),
        grid=(tokens // tb,),
        in_specs=[rows, fixed((experts * head, width)), cols2],
        out_specs=[spec((2, head, tb), lambda i: (0, 0, i)), spec((2, tb, LANES), lambda i: (0, i, 0))],
        out_shape=[shape((2, head, tokens), BF), shape((2, tokens, LANES), BF)],
        compiler_params=PARAMS,
        cost_estimate=cost(5),
    )(normed, wq, routes_t)
    feed = jnp.concatenate(
        [expand_weight, reduce_weight, jnp.broadcast_to(expand_bias[None], (16, units)), o_share],
        axis=0,
    )
    feed, pair_across, queries = lax.optimization_barrier((feed, pair_across, queries))
    pair = (pairs, pair_beside, pair_across, swapped(pair_across, 1))
    feed_across = swapped(feed, 2)

    tq = 512
    att, kept = pl.pallas_call(
        functools.partial(attend_kernel, head=head, span=4 * tokens),
        grid=(2, tokens // tq),
        in_specs=[SMEM, SMEM, spec((1, head, tq), lambda s, i: (s, 0, i))] + [fixed((tokens, 2 * head))] * 4,
        out_specs=[spec((1, head + 8, tq), lambda s, i: (s, 0, i)),
                   spec((4 * tokens, tq), lambda s, i: (0, s * (tokens // tq) + i))],
        out_shape=[shape((2, head + 8, tokens), F32), shape((4 * tokens, 2 * tokens), BF)],
        scratch_shapes=[
            pltpu.VMEM((4 * tokens, LANES), BF), pltpu.VMEM((LANES, 4 * tokens), BF),
            pltpu.VMEM((8, LANES), F32), pltpu.VMEM((8, tq), F32),
        ],
        compiler_params=PARAMS,
        cost_estimate=cost(33),
    )(owners, lengths, queries, *pair)

    feed_across = tied(feed_across, att)
    feeds = (feed, swapped(feed, 1), feed_across, swapped(feed_across, 1))

    tm = 512
    rows = spec((tm, width), lambda i: (i, 0))
    cols2 = spec((2, tm), lambda i: (0, i))
    tail = 2 * width + 64
    share = experts * head // 4
    slot = tail + share
    both_rows = spec((2, tm, LANES), lambda i: (0, i, 0))
    both_cols = spec((2, LANES, tm), lambda i: (0, 0, i))
    att_cols = spec((2, head + 8, tm), lambda i: (0, 0, i))
    active, middle, mid_grad, do_rows, do_t, logit, *ffn = pl.pallas_call(
        functools.partial(middle_kernel, head=head, experts=experts),
        grid=(tokens // tm,),
        in_specs=[SMEM, att_cols, cols2, cols2, rows, rows, rows]
        + [fixed(feed.shape)] * 4 + [fixed((1, width))] * 2,
        out_specs=[spec((tm, 4 * units), lambda i: (i, 0)), rows, rows, both_rows, both_cols, spec((16, tm), lambda i: (0, i))]
        + [fixed((slot, units))] * 4,
        out_shape=[shape((tokens, 4 * units), BF), shape((tokens, width), BF), shape((tokens, width), BF),
                   shape((2, tokens, LANES), BF), shape((2, LANES, tokens), BF), shape((16, tokens), BF)]
        + [shape((slot, units), BF)] * 4,
        scratch_shapes=[
            pltpu.VMEM((width, 4 * units), F32), pltpu.VMEM((width, 4 * units), F32),
            pltpu.VMEM((experts * head, width), F32), pltpu.VMEM((8, 4 * units), F32),
            pltpu.VMEM((8, width), F32), pltpu.VMEM((16, width), F32),
            pltpu.VMEM((experts * head, width), BF),
        ],
        compiler_params=PARAMS,
        cost_estimate=cost(50),
    )(owners, att, routes_t, gates, x, up, normed, *feeds, gain2, bias2)

    half = tokens // 2

    def back_call(places, before, us, carried=None):
        carry = carried is not None
        ends = [size for _, _, size in places]
        ends[0] += carried.shape[0] if carry else 0
        many = sum(size for _, _, size in places)
        first = before is None
        tq = half if many <= half else 512
        per = tokens // tq
        row_block = spec((1, tq, LANES), lambda i: (i // per, i % per, 0))
        col_block = spec((1, LANES, tq), lambda i: (i // per, 0, i % per))
        grad_block = spec((1, head, tq), lambda i: (i // per, 0, i % per))
        return pl.pallas_call(
            functools.partial(attend_back_kernel, head=head, places=places, first=first, carry=carry),
            grid=(2 * per,),
            in_specs=[col_block, row_block, row_block] + [grad_block] * (not first)
            + [fixed(carried.shape) for _ in range(carry)]
            + [spec((size, tq), lambda i, at=o * tokens // size + at: (at, i)) for o, at, size in places]
            + [spec((size, 2 * head), lambda i, at=at: (at, 0)) for _, at, size in places],
            out_specs=[grad_block] + [fixed((size, 2 * head)) for size in ends],
            out_shape=[shape((2, head, tokens), F32)]
            + [shape((size, 2 * head), BF) for size in ends],
            input_output_aliases={} if first else {3: 0},
            scratch_shapes=[
                pltpu.VMEM((many, LANES), BF), pltpu.VMEM((head, many), BF),
                pltpu.VMEM((many, LANES), F32),
            ],
            compiler_params=PARAMS,
            cost_estimate=cost(us),
        )(do_t, do_rows, q_rows, *([] if first else [before]), *([carried] if carry else []), *[kept] * len(places),
          *[pair[o] for o, _, _ in places])

    def by_holder(rows_of):
        each = rows_of.reshape(experts, head // 4, dp // experts, -1).transpose(0, 2, 1, 3)
        return each.reshape(dp, -1, width)

    from3, from1 = swapped(ffn[3], 1), swapped(ffn[1], 1)
    q_grad, key3a = back_call([(3, 0, half)], None, 11)
    far, near = summed(ffn[2], from3), summed(ffn[0], from1)
    q_grad, far, near = lax.optimization_barrier((q_grad, far, near))
    from2 = swapped(far, 2)
    q_grad, key3, key2 = back_call([(3, 1, half), (2, 0, tokens)], q_grad, 30, key3a)
    own = summed(near, from2)
    own = jnp.concatenate([own[:tail].reshape(dp, -1, width), by_holder(own[tail:])], axis=1)
    q_grad, own, key3, key2 = lax.optimization_barrier((q_grad, own, key3, key2))
    arrived = lax.all_to_all(own, "dp", split_axis=0, concat_axis=0, tiled=True)
    key_from3, key_from2 = swapped(key3, 3), swapped(key2, 2)
    q_grad, key1, key0 = back_call([(1, 0, tokens), (0, 0, tokens)], q_grad, 39)
    piece = jnp.sum(arrived.astype(F32), axis=0)
    q_grad, piece, key1 = lax.optimization_barrier((q_grad, piece, key1))
    key_from1 = swapped(key1, 1)
    total = sent_to_all(piece[: tail // dp].astype(BF), "dp").reshape(tail, units)
    wo_total = piece[tail // dp :].reshape(head // 4, -1)

    tl = 512
    rows = spec((tl, width), lambda i: (i, 0))
    cols2 = spec((2, tl), lambda i: (0, i))
    pair_rows = spec((tl, 2 * head), lambda i: (i, 0))
    normed_grad, *last = pl.pallas_call(
        functools.partial(last_kernel, head=head, experts=experts, scale=0.125),
        grid=(tokens // tl,),
        in_specs=[SMEM, spec((2, head, tl), lambda i: (0, 0, i)), pair_rows, pair_rows, pair_rows, pair_rows,
                  spec((16, tl), lambda i: (0, i)), cols2, rows, rows,
                  fixed((experts * head, width)), fixed((width, 2 * head)), fixed((2 * experts, width))],
        out_specs=[rows] + [fixed((share + 48, width))] * 4,
        out_shape=[shape((tokens, width), BF)] + [shape((share + 48, width), BF)] * 4,
        scratch_shapes=[
            pltpu.VMEM((experts * head, width), F32), pltpu.VMEM((2 * head, width), F32),
            pltpu.VMEM((8, width), F32),
        ],
        compiler_params=PARAMS,
        cost_estimate=cost(10),
    )(owners, q_grad, key0, key_from1, key_from2, key_from3, logit, routes_t, normed, x, wq,
      shared_proj, router_t)

    near, far = summed(last[0], swapped(last[1], 1)), summed(last[2], swapped(last[3], 1))
    from2 = swapped(far, 2)
    normed_grad, active, near = lax.optimization_barrier((normed_grad, active, near))
    to = 512
    rows = spec((to, width), lambda i: (i, 0))
    block_out, input_grad = pl.pallas_call(
        outputs_kernel,
        grid=(tokens // to,),
        in_specs=[spec((to, 4 * units), lambda i: (i, 0)), rows]
        + [spec((units, width), lambda i: (width // units, 0))] * 4
        + [fixed((1, width)), rows, rows, rows, fixed((1, width))],
        out_specs=[rows, rows],
        out_shape=[shape((tokens, width), BF), shape((tokens, width), F32)],
        compiler_params=PARAMS,
        cost_estimate=cost(10),
    )(active, middle, *feeds, reduce_bias[None].astype(F32), normed_grad, x, mid_grad, gain1)
    mine, total, input_grad = lax.optimization_barrier((summed(near, from2), total, input_grad))
    total = total.astype(F32)
    ends = jnp.broadcast_to(mine[share : share + 40][None], (dp, 40, width))
    each = jnp.concatenate([by_holder(mine[:share]), ends], axis=1)
    got = lax.all_to_all(each, "dp", split_axis=0, concat_axis=0, tiled=True)
    got = jnp.sum(got.astype(F32), axis=0)
    wq_total = got[: share // dp].reshape(head // 4, -1)
    ends = got[share // dp :]
    block = width // 4
    each = 2 * head // 4
    shared_total = jnp.concatenate(
        [ends[:each, g * block : (g + 1) * block] for g in range(4)], axis=0
    )
    cut = lax.dynamic_slice_in_dim(total[2 * width : 2 * width + 16], me * block, block, axis=1)
    return (
        block_out.reshape(1, tokens, width),
        input_grad.reshape(1, tokens, width),
        ends[each, :block],
        ends[each, block : 2 * block],
        cut[8 : 8 + experts].T,
        shared_total.T,
        wq_total,
        wo_total,
        cut[1],
        cut[2],
        total[:width],
        total[2 * width + 3],
        total[width : 2 * width].T,
        cut[0],
    )


def solution(mesh):
    both = P("dp", "mp", None)
    table = P("mp", "dp")
    placed = (
        both, both, P("dp"), P(), P(), P(), P(), table, table, P(), P(), P(None, "mp"), P("mp"),
        P("mp", None), P(), both,
    )
    given = (
        both, both, P("mp"), P("mp"), P("mp", None), P("mp", None), table, table, P("mp"), P("mp"),
        P(None, "mp"), P("mp"), P("mp", None), P("mp"),
    )
    return jax.shard_map(on_device, mesh=mesh, in_specs=placed, out_specs=given, check_vma=False)
```

```python
import functools

import jax
import jax.numpy as jnp
from jax import lax
from jax.experimental import pallas as pl
from jax.experimental.pallas import tpu as pltpu
from jax.sharding import PartitionSpec as P

F32 = jnp.float32
BF = jnp.bfloat16
EPS = 1e-05
SCALE = 0.125
TO_EXP2 = SCALE * 1.4426950408889634
MASKED = -1e30
GELU_A = 0.7978845608028654
GELU_B = 0.044715
SAFE = 60.0
LANES = 128


def nn(a, b):
    return lax.dot_general(a, b, (((1,), (0,)), ((), ())), preferred_element_type=F32)


def nt(a, b):
    return lax.dot_general(a, b, (((1,), (1,)), ((), ())), preferred_element_type=F32)


def tn(a, b):
    return lax.dot_general(a, b, (((0,), (0,)), ((), ())), preferred_element_type=F32)


def norm_parts(values):
    centred = values - jnp.mean(values, axis=-1, keepdims=True)
    inverse = lax.rsqrt(jnp.mean(centred * centred, axis=-1, keepdims=True) + EPS)
    return centred * inverse, inverse


def norm_back(grad, normal, inverse, gain):
    scaled = grad * gain
    return inverse * (
        scaled
        - jnp.mean(scaled, axis=-1, keepdims=True)
        - normal * jnp.mean(scaled * normal, axis=-1, keepdims=True)
    )


def three(value):
    high = value.astype(BF).astype(F32)
    rest = value - high
    middle = rest.astype(BF).astype(F32)
    return high, middle, rest - middle


def extra_rows(value, last):
    row = lax.broadcasted_iota(jnp.int32, (16, value.shape[1]), 0)
    high, middle, low = three(value)
    out = jnp.where(row == 0, -high, 0.0)
    out = jnp.where(row == 1, -middle, out)
    out = jnp.where(row == 2, -low, out)
    return jnp.where(row == 3, last, out)


def spread(first, second, route0, route1, experts):
    zero = jnp.zeros_like(first)
    return jnp.concatenate(
        [
            jnp.where(route0 == e, first, jnp.where(route1 == e, second, zero))
            for e in range(experts)
        ],
        axis=0,
    )


def picked(table, route, experts):
    head = table.shape[0] // experts
    out = jnp.zeros((head, table.shape[1]), F32)
    for e in range(experts):
        out = jnp.where(route == e, table[e * head : (e + 1) * head, :], out)
    return out


def key_rows(pair, live, head):
    lane = lax.broadcasted_iota(jnp.int32, pair.shape, 1)
    row = lax.broadcasted_iota(jnp.int32, pair.shape, 0)
    ones = jnp.where(lane < head + 3, 1.0, 0.0)
    mask = jnp.where(row < live, 0.0, MASKED)
    out = jnp.where(lane == head + 3, mask, ones)
    return jnp.where(lane < head, pair.astype(F32), out).astype(BF)


def first_kernel(x, gain, bias, router, proj, routes, normed, pairs, gates):
    experts = router.shape[0] // 2
    normal, _ = norm_parts(x[...].astype(F32))
    out = (normal * gain[...] + bias[...]).astype(BF)
    normed[...] = out
    pairs[...] = nn(out, proj[...]).astype(BF)
    logits = nt(router[...], out)
    route = routes[...]
    chosen = []
    for s in range(2):
        one = jnp.zeros((1, logits.shape[1]), F32)
        for e in range(experts):
            one = jnp.where(route[s : s + 1, :] == e, logits[e : e + 1, :], one)
        chosen.append(one)
    top = jnp.maximum(chosen[0], chosen[1])
    up0, up1 = jnp.exp(chosen[0] - top), jnp.exp(chosen[1] - top)
    inverse = 1.0 / (up0 + up1)
    gates[0:1, :] = up0 * inverse
    gates[1:2, :] = up1 * inverse


def query_kernel(normed, table, routes, queries, q_rows, *, experts):
    every = nt(table[...], normed[...])
    for s in range(2):
        one = picked(every, routes[s : s + 1, :], experts)
        queries[s] = one.astype(BF)
        q_rows[s] = jnp.concatenate([one, jnp.zeros_like(one)], axis=0).T.astype(BF)


def assembled(table, shares, where, experts, start):
    head = table.shape[0] // experts
    share = head // 4
    for o, part in enumerate(shares):
        for e in range(experts):
            at = pl.multiple_of(e * head + where[o] * share, share)
            here = slice(start + e * share, start + (e + 1) * share)
            table[pl.ds(at, share), :] = part[here, :]


def attend_kernel(where, length, q, p0, p1, p2, p3, out, kept, keys, values, limit, top, *, head, span):
    part = p0.shape[0]

    @pl.when((pl.program_id(0) == 0) & (pl.program_id(1) == 0))
    def _():
        row = lax.broadcasted_iota(jnp.int32, (LANES, LANES), 0)
        col = lax.broadcasted_iota(jnp.int32, (LANES, LANES), 1)
        move = jnp.where((col == row + head) & (row < head), 1.0, 0.0).astype(BF)
        count = jnp.where(row < head, 1.0, 0.0).astype(BF)
        longest = jnp.zeros((1, LANES), F32)
        for o, p in enumerate((p0, p1, p2, p3)):
            pair = p[...]
            live = length[0] - where[o] * part
            keys[o * part : (o + 1) * part, :] = key_rows(pair, live, head)
            turned = nt(move, pair)
            line = lax.broadcasted_iota(jnp.int32, turned.shape, 0)
            values[:, o * part : (o + 1) * part] = jnp.where(line == head, 1.0, turned).astype(BF)
            wide = pair.astype(F32)
            squares = nn((wide * wide).astype(BF), count)
            longest = jnp.maximum(longest, jnp.max(squares, axis=0, keepdims=True))
        limit[...] = jnp.broadcast_to(1.02 * jnp.sqrt(longest), limit.shape)

    query = q[0]
    wide = query.astype(F32)
    length = jnp.sqrt(jnp.sum(wide * wide, axis=0, keepdims=True))
    bound = length * limit[0:1, 0:1] * TO_EXP2
    top[...] = jnp.zeros_like(top)
    n = query.shape[1]
    rest = jnp.zeros((LANES - head - 16, n), BF)

    @pl.when(jnp.max(bound) > SAFE)
    def _():
        plain = jnp.concatenate(
            [query, extra_rows(jnp.zeros((1, n), F32), 1.0).astype(BF), rest], axis=0
        )

        def peak(j, now):
            at = pl.multiple_of(j * 512, 512)
            scores = nn(keys[pl.ds(at, 512), :], plain)
            return jnp.maximum(now, jnp.max(scores, axis=0, keepdims=True))

        best = lax.fori_loop(0, 4 * part // 512, peak, jnp.full((1, n), -3e38, F32))
        top[...] = jnp.broadcast_to(best, top.shape)

    extended = jnp.concatenate([query, extra_rows(top[0:1, :], 1.0).astype(BF), rest], axis=0)
    total = jnp.zeros((LANES, n), F32)
    for j in range(4 * part // span):
        here = slice(j * span, (j + 1) * span)
        weights = jnp.exp2(nn(keys[here, :], extended) * TO_EXP2).astype(BF)
        kept[here, :] = weights
        total = total + nn(values[:, here], weights)
    inverse = 1.0 / total[head : head + 1, :]
    out[0, 0:head, :] = total[0:head, :] * inverse
    out[0, head : head + 8, :] = jnp.broadcast_to(inverse, (8, n))


def attend_back_kernel(dot, do, q, *rest, head, places, first, carry):
    if not first:
        before, *rest = rest
    if carry:
        carried, *rest = rest
    pieces = len(places)
    weights, pairs, after = rest[:pieces], rest[pieces : 2 * pieces], rest[2 * pieces]
    grads = rest[2 * pieces + 1 : 3 * pieces + 1]
    values, turned, both = rest[3 * pieces + 1 :]
    step = pl.program_id(0)
    sizes = [pair.shape[0] for pair in pairs]
    spans = [slice(sum(sizes[:n]), sum(sizes[: n + 1])) for n in range(pieces)]

    @pl.when(step == 0)
    def _():
        row = lax.broadcasted_iota(jnp.int32, (head, LANES), 0)
        col = lax.broadcasted_iota(jnp.int32, (head, LANES), 1)
        same = jnp.where(row == col, 1.0, 0.0).astype(BF)
        for pair, here in zip(pairs, spans):
            rows = pair[...]
            turned[:, here] = nt(same, rows).astype(BF)
            lane = lax.broadcasted_iota(jnp.int32, rows.shape, 1)
            fixed = jnp.where(lane < 3, 1.0, 0.0)
            values[here, :] = jnp.where(lane < head, fixed, rows.astype(F32)).astype(BF)
        both[...] = jnp.zeros_like(both)

    right = jnp.concatenate([q[0], do[0]], axis=0)
    grown = jnp.zeros((head, q.shape[1]), F32)
    for weight, here in zip(weights, spans):
        attention = weight[...]
        scores = (attention.astype(F32) * nn(values[here, :], dot[0])).astype(BF)
        both[here, :] += nn(jnp.concatenate([scores, attention], axis=1), right)
        grown = grown + nn(turned[:, here], scores)
    after[0] = grown if first else before[0] + grown

    @pl.when(step == pl.num_programs(0) - 1)
    def _():
        for n, (grad, here) in enumerate(zip(grads, spans)):
            at = 0
            if carry and n == 0:
                at = carried.shape[0]
                grad[0:at, :] = carried[...]
            size = sizes[n]
            lane = lax.broadcasted_iota(jnp.int32, (size, LANES), 1)
            grad[at : at + size, :] = (both[here, :] * jnp.where(lane < head, SCALE, 1.0)).astype(BF)


def middle_kernel(
    where, att, routes, gates, x, up, normed,
    f0, f1, f2, f3, gain, bias,
    active, kept, mid_grad, do_rows, do_t, logit, g0, g1, g2, g3,
    we_sum, wr_sum, wo_sum, eb_sum, small, rt_sum, wo,
    *, head, experts,
):
    step = pl.program_id(0)

    @pl.when(step == 0)
    def _():
        for r in (we_sum, wr_sum, wo_sum, eb_sum, small, rt_sum):
            r[...] = jnp.zeros_like(r)
        assembled(wo, (f0, f1, f2, f3), where, experts, f0.shape[0] - experts * (head // 4))

    route0, route1 = routes[0:1, :], routes[1:2, :]
    gate0, gate1 = gates[0:1, :], gates[1:2, :]
    mix0, mix1 = att[0, 0:head, :], att[1, 0:head, :]
    low0, low1 = mix0.astype(BF).astype(F32), mix1.astype(BF).astype(F32)
    mixed = spread(gate0 * low0, gate1 * low1, route0, route1, experts).astype(BF)
    middle = x[...].astype(F32) + tn(mixed, wo[...])
    normal, inverse = norm_parts(middle)
    normed_two = (normal * gain[...] + bias[...]).astype(BF)
    upstream = up[...]
    n2t = normed_two.T
    upt = upstream.T
    ff = f0.shape[1]
    width = middle.shape[1]
    two_grad = jnp.zeros(middle.shape, F32)
    backs = []
    for o, f in enumerate((f0, f1, f2, f3)):
        here = slice(o * ff, (o + 1) * ff)
        v = nn(normed_two, f[0:width, :])
        v = v + f[width + ff : width + ff + 16, :].astype(F32)[0:1, :]
        square = v * v
        inner = v * (GELU_A + (GELU_A * GELU_B) * square)
        half = 0.5 + 0.5 * jnp.tanh(inner)
        act = v * half
        slope = half + act * (1.0 - half) * (2.0 * GELU_A + (6.0 * GELU_A * GELU_B) * square)
        active[:, here] = act.astype(BF)
        backs.append((nt(upstream, f[width : width + ff, :]) * slope).astype(BF))
    for o, f in enumerate((f0, f1, f2, f3)):
        here = slice(o * ff, (o + 1) * ff)
        back = backs[o]
        two_grad = two_grad + nt(back, f[0:width, :])
        we_sum[:, here] += nn(n2t, back)
        wr_sum[:, here] += nn(upt, active[:, here])
        eb_sum[0:1, here] += jnp.sum(back.astype(F32), axis=0, keepdims=True)
    kept[...] = middle.astype(BF)
    wide_up = upstream.astype(F32)
    mid = wide_up + norm_back(two_grad, normal, inverse, gain[...])
    mid_grad[...] = mid.astype(BF)
    small[0:1, :] += jnp.sum(wide_up, axis=0, keepdims=True)
    small[1:2, :] += jnp.sum(two_grad * normal, axis=0, keepdims=True)
    small[2:3, :] += jnp.sum(two_grad, axis=0, keepdims=True)
    mid_low = mid.astype(BF)
    wo_sum[...] += nn(mixed, mid_low)
    every = nt(wo[...], mid_low)
    pull0, pull1 = picked(every, route0, experts), picked(every, route1, experts)
    gate_grad0 = jnp.sum(low0 * pull0, axis=0, keepdims=True)
    gate_grad1 = jnp.sum(low1 * pull1, axis=0, keepdims=True)
    both = gate0 * gate_grad0 + gate1 * gate_grad1
    chosen0, chosen1 = gate0 * (gate_grad0 - both), gate1 * (gate_grad1 - both)
    row = lax.broadcasted_iota(jnp.int32, (16, chosen0.shape[1]), 0)
    logit_rows = jnp.where(row == route0, chosen0, jnp.where(row == route1, chosen1, 0.0))
    logit_high = logit_rows.astype(BF)
    logit_low = (logit_rows - logit_high.astype(F32)).astype(BF)
    logit[...] = logit_high
    here_normed = normed[...]
    rt_sum[...] += nn(logit_high, here_normed) + nn(logit_low, here_normed)
    rest = jnp.zeros((LANES - head - 16, row.shape[1]), F32)
    for s, (gate, pull, mix) in enumerate(((gate0, pull0, mix0), (gate1, pull1, mix1))):
        low = (gate * pull * att[s, head : head + 1, :]).astype(BF)
        grad = low.astype(F32)
        delta = jnp.sum(grad * mix, axis=0, keepdims=True)
        do_t[s] = jnp.concatenate([extra_rows(delta, 0.0), rest, grad], axis=0).astype(BF)
        do_rows[s] = jnp.concatenate([jnp.zeros_like(grad), grad], axis=0).T.astype(BF)

    @pl.when(step == pl.num_programs(0) - 1)
    def _():
        share = head // 4
        table = g0.shape[0] - experts * share
        for o, g in enumerate((g0, g1, g2, g3)):
            here = slice(o * ff, (o + 1) * ff)
            g[0:width, :] = we_sum[:, here].astype(BF)
            g[width : 2 * width, :] = wr_sum[:, here].astype(BF)
            line = lax.broadcasted_iota(jnp.int32, (8, ff), 0)
            head_rows = jnp.where(line == 3, eb_sum[0:1, here], small[...])
            g[2 * width : 2 * width + 16, :] = jnp.concatenate(
                [head_rows, rt_sum[0:8, :]], axis=0
            ).astype(BF)
            g[2 * width + 16 : table, :] = jnp.zeros((table - 2 * width - 16, ff), BF)
            for e in range(experts):
                at = pl.multiple_of(e * head + where[o] * share, share)
                g[table + e * share : table + (e + 1) * share, :] = wo_sum[
                    pl.ds(at, share), :
                ].astype(BF)


def last_kernel(
    where, dq, p0, p1, p2, p3, logit, routes, normed, x, wq, proj, router,
    out, s0, s1, s2, s3, wq_sum, sp_sum, small, *, head, experts,
):
    step = pl.program_id(0)

    @pl.when(step == 0)
    def _():
        for r in (wq_sum, sp_sum, small):
            r[...] = jnp.zeros_like(r)

    route0, route1 = routes[0:1, :], routes[1:2, :]
    grad0, grad1 = dq[0] * SCALE, dq[1] * SCALE
    placed = spread(grad0, grad1, route0, route1, experts).astype(BF)
    own = p0[...].astype(F32)
    for p in (p1, p2, p3):
        own = own + p[...].astype(F32)
    pair = own.astype(BF)
    normed_grad = tn(placed, wq[...]) + nt(pair, proj[...]) + tn(logit[...], router[...])
    here_normed = normed[...]
    wq_sum[...] += nn(placed, here_normed)
    sp_sum[...] += tn(pair, here_normed)
    normal, _ = norm_parts(x[...].astype(F32))
    out[...] = normed_grad.astype(BF)
    small[0:1, :] += jnp.sum(normed_grad * normal, axis=0, keepdims=True)
    small[1:2, :] += jnp.sum(normed_grad, axis=0, keepdims=True)

    @pl.when(step == pl.num_programs(0) - 1)
    def _():
        share = head // 4
        block = sp_sum.shape[1] // 4
        each = sp_sum.shape[0] // 4
        table = experts * share
        for o, s in enumerate((s0, s1, s2, s3)):
            owner = where[o]
            for e in range(experts):
                at = pl.multiple_of(e * head + owner * share, share)
                s[e * share : (e + 1) * share, :] = wq_sum[pl.ds(at, share), :].astype(BF)
            lanes = pl.ds(pl.multiple_of(owner * block, block), block)
            s[table + each : table + each + 16, :] = jnp.zeros((16, 4 * block), BF)
            line = lax.broadcasted_iota(jnp.int32, (16, block), 0)
            for g in range(2):
                ends = jnp.where(line == 0, small[g : g + 1, lanes], 0.0)
                s[table + each : table + each + 16, g * block : (g + 1) * block] = ends.astype(BF)
            for g in range(4):
                piece = sp_sum[g * each : (g + 1) * each, lanes]
                s[table : table + each, g * block : (g + 1) * block] = piece.astype(BF)


def outputs_kernel(active, middle, r0, r1, r2, r3, rb, normed_grad, x, mid_grad, gain, out, x_grad):
    ff = r0.shape[0]
    total = middle[...].astype(F32) + rb[...]
    for o, r in enumerate((r0, r1, r2, r3)):
        total = total + nn(active[:, o * ff : (o + 1) * ff], r[...])
    out[...] = total.astype(BF)
    normal, inverse = norm_parts(x[...].astype(F32))
    back = norm_back(normed_grad[...].astype(F32), normal, inverse, gain[...])
    x_grad[...] = mid_grad[...].astype(F32) + back


def swapped(value, bit):
    return lax.ppermute(value, "mp", [(i, i ^ bit) for i in range(4)])


def four(value):
    across = swapped(value, 2)
    return value, swapped(value, 1), across, swapped(across, 1)


def summed(a, b):
    return (a.astype(F32) + b.astype(F32)).astype(BF)


def sent_to_all(value, axes):
    n = lax.axis_size(axes)
    wide = jnp.broadcast_to(value[None], (n,) + value.shape)
    return lax.all_to_all(wide, axes, split_axis=0, concat_axis=0, tiled=True)


def whole_table(share, experts):
    dp, mp = lax.axis_size("dp"), lax.axis_size("mp")
    rows, cols = share.shape
    every = sent_to_all(share, ("dp", "mp"))
    each = every.reshape(experts, dp // experts, mp, rows, cols)
    return each.transpose(0, 2, 3, 1, 4).reshape(experts * mp * rows, dp // experts * cols)


def spec(shape, index):
    return pl.BlockSpec(shape, index)


def fixed(shape):
    return pl.BlockSpec(shape, lambda *_: (0,) * len(shape))


def shape(dims, kind):
    return jax.ShapeDtypeStruct(dims, kind)


SMEM = pl.BlockSpec(memory_space=pltpu.SMEM)
PARAMS = pltpu.CompilerParams(vmem_limit_bytes=58 * 2**20)


def cost(us):
    return pl.CostEstimate(flops=int(us * 1.1e9), bytes_accessed=1024, transcendentals=0)


def tied(value, *others):
    return lax.optimization_barrier((value, *others))[0]


def on_device(
    block_input, routes, lengths, first_gain, first_bias, router_weight, shared_proj,
    query_weight, output_weight, second_gain, second_bias, expand_weight, expand_bias,
    reduce_weight, reduce_bias, upstream_grad,
):
    tokens, width = block_input.shape[1], block_input.shape[2]
    experts = router_weight.shape[1]
    head = query_weight.shape[0] * lax.axis_size("mp")
    dp = lax.axis_size("dp")
    units = expand_weight.shape[1]
    me = lax.axis_index("mp")
    owners = me ^ jnp.arange(4, dtype=jnp.int32)
    x = block_input.reshape(tokens, width)
    up = upstream_grad.reshape(tokens, width)
    routes_t = routes.reshape(tokens, 2).T
    router_t = jnp.pad(router_weight.T, ((0, experts), (0, 0)))
    gain1, bias1 = first_gain[None], first_bias[None]
    gain2, bias2 = second_gain[None], second_bias[None]

    wq = whole_table(query_weight, experts)

    tb = 512
    rows = spec((tb, width), lambda i: (i, 0))
    cols2 = spec((2, tb), lambda i: (0, i))
    normed, pairs, gates = pl.pallas_call(
        first_kernel,
        grid=(tokens // tb,),
        in_specs=[rows, fixed((1, width)), fixed((1, width)), fixed((2 * experts, width)),
                  fixed((width, 2 * head)), cols2],
        out_specs=[rows, spec((tb, 2 * head), lambda i: (i, 0)), cols2],
        out_shape=[shape((tokens, width), BF), shape((tokens, 2 * head), BF), shape((2, tokens), F32)],
        compiler_params=PARAMS,
        cost_estimate=cost(5),
    )(x, gain1, bias1, router_t, shared_proj, routes_t)

    pair_across = swapped(pairs, 2)
    pair_beside = swapped(pairs, 1)
    output_weight, wq = lax.optimization_barrier((output_weight, wq))
    o_share = sent_to_all(output_weight, "dp")
    o_share = o_share.reshape(experts, dp // experts, head // 4, -1).transpose(0, 2, 1, 3)
    o_share = o_share.reshape(experts * head // 4, width)
    queries, q_rows = pl.pallas_call(
        functools.partial(query_kernel, experts=experts),
        grid=(tokens // tb,),
        in_specs=[rows, fixed((experts * head, width)), cols2],
        out_specs=[spec((2, head, tb), lambda i: (0, 0, i)), spec((2, tb, LANES), lambda i: (0, i, 0))],
        out_shape=[shape((2, head, tokens), BF), shape((2, tokens, LANES), BF)],
        compiler_params=PARAMS,
        cost_estimate=cost(5),
    )(normed, wq, routes_t)
    feed = jnp.concatenate(
        [expand_weight, reduce_weight, jnp.broadcast_to(expand_bias[None], (16, units)), o_share],
        axis=0,
    )
    feed, pair_across, queries = lax.optimization_barrier((feed, pair_across, queries))
    pair = (pairs, pair_beside, pair_across, swapped(pair_across, 1))
    feed_across = swapped(feed, 2)

    tq = 512
    att, kept = pl.pallas_call(
        functools.partial(attend_kernel, head=head, span=4 * tokens),
        grid=(2, tokens // tq),
        in_specs=[SMEM, SMEM, spec((1, head, tq), lambda s, i: (s, 0, i))] + [fixed((tokens, 2 * head))] * 4,
        out_specs=[spec((1, head + 8, tq), lambda s, i: (s, 0, i)),
                   spec((4 * tokens, tq), lambda s, i: (0, s * (tokens // tq) + i))],
        out_shape=[shape((2, head + 8, tokens), F32), shape((4 * tokens, 2 * tokens), BF)],
        scratch_shapes=[
            pltpu.VMEM((4 * tokens, LANES), BF), pltpu.VMEM((LANES, 4 * tokens), BF),
            pltpu.VMEM((8, LANES), F32), pltpu.VMEM((8, tq), F32),
        ],
        compiler_params=PARAMS,
        cost_estimate=cost(33),
    )(owners, lengths, queries, *pair)

    feed_across = tied(feed_across, att)
    feeds = (feed, swapped(feed, 1), feed_across, swapped(feed_across, 1))

    tm = 512
    rows = spec((tm, width), lambda i: (i, 0))
    cols2 = spec((2, tm), lambda i: (0, i))
    tail = 2 * width + 64
    share = experts * head // 4
    slot = tail + share
    both_rows = spec((2, tm, LANES), lambda i: (0, i, 0))
    both_cols = spec((2, LANES, tm), lambda i: (0, 0, i))
    att_cols = spec((2, head + 8, tm), lambda i: (0, 0, i))
    active, middle, mid_grad, do_rows, do_t, logit, *ffn = pl.pallas_call(
        functools.partial(middle_kernel, head=head, experts=experts),
        grid=(tokens // tm,),
        in_specs=[SMEM, att_cols, cols2, cols2, rows, rows, rows]
        + [fixed(feed.shape)] * 4 + [fixed((1, width))] * 2,
        out_specs=[spec((tm, 4 * units), lambda i: (i, 0)), rows, rows, both_rows, both_cols, spec((16, tm), lambda i: (0, i))]
        + [fixed((slot, units))] * 4,
        out_shape=[shape((tokens, 4 * units), BF), shape((tokens, width), BF), shape((tokens, width), BF),
                   shape((2, tokens, LANES), BF), shape((2, LANES, tokens), BF), shape((16, tokens), BF)]
        + [shape((slot, units), BF)] * 4,
        scratch_shapes=[
            pltpu.VMEM((width, 4 * units), F32), pltpu.VMEM((width, 4 * units), F32),
            pltpu.VMEM((experts * head, width), F32), pltpu.VMEM((8, 4 * units), F32),
            pltpu.VMEM((8, width), F32), pltpu.VMEM((16, width), F32),
            pltpu.VMEM((experts * head, width), BF),
        ],
        compiler_params=PARAMS,
        cost_estimate=cost(50),
    )(owners, att, routes_t, gates, x, up, normed, *feeds, gain2, bias2)

    half = tokens // 2

    def back_call(places, before, us, carried=None):
        carry = carried is not None
        ends = [size for _, _, size in places]
        ends[0] += carried.shape[0] if carry else 0
        many = sum(size for _, _, size in places)
        first = before is None
        tq = half if many <= half else 512
        per = tokens // tq
        row_block = spec((1, tq, LANES), lambda i: (i // per, i % per, 0))
        col_block = spec((1, LANES, tq), lambda i: (i // per, 0, i % per))
        grad_block = spec((1, head, tq), lambda i: (i // per, 0, i % per))
        return pl.pallas_call(
            functools.partial(attend_back_kernel, head=head, places=places, first=first, carry=carry),
            grid=(2 * per,),
            in_specs=[col_block, row_block, row_block] + [grad_block] * (not first)
            + [fixed(carried.shape) for _ in range(carry)]
            + [spec((size, tq), lambda i, at=o * tokens // size + at: (at, i)) for o, at, size in places]
            + [spec((size, 2 * head), lambda i, at=at: (at, 0)) for _, at, size in places],
            out_specs=[grad_block] + [fixed((size, 2 * head)) for size in ends],
            out_shape=[shape((2, head, tokens), F32)]
            + [shape((size, 2 * head), BF) for size in ends],
            input_output_aliases={} if first else {3: 0},
            scratch_shapes=[
                pltpu.VMEM((many, LANES), BF), pltpu.VMEM((head, many), BF),
                pltpu.VMEM((many, LANES), F32),
            ],
            compiler_params=PARAMS,
            cost_estimate=cost(us),
        )(do_t, do_rows, q_rows, *([] if first else [before]), *([carried] if carry else []), *[kept] * len(places),
          *[pair[o] for o, _, _ in places])

    def by_holder(rows_of):
        each = rows_of.reshape(experts, head // 4, dp // experts, -1).transpose(0, 2, 1, 3)
        return each.reshape(dp, -1, width)

    from3, from1 = swapped(ffn[3], 1), swapped(ffn[1], 1)
    q_grad, key3a = back_call([(3, 0, half)], None, 11)
    far, near = summed(ffn[2], from3), summed(ffn[0], from1)
    q_grad, far, near = lax.optimization_barrier((q_grad, far, near))
    from2 = swapped(far, 2)
    q_grad, key3, key2 = back_call([(3, 1, half), (2, 0, tokens)], q_grad, 30, key3a)
    own = summed(near, from2)
    own = jnp.concatenate([own[:tail].reshape(dp, -1, width), by_holder(own[tail:])], axis=1)
    q_grad, own, key3, key2 = lax.optimization_barrier((q_grad, own, key3, key2))
    arrived = lax.all_to_all(own, "dp", split_axis=0, concat_axis=0, tiled=True)
    key_from3, key_from2 = swapped(key3, 3), swapped(key2, 2)
    q_grad, key1, key0 = back_call([(1, 0, tokens), (0, 0, tokens)], q_grad, 39)
    piece = jnp.sum(arrived.astype(F32), axis=0)
    q_grad, piece, key1 = lax.optimization_barrier((q_grad, piece, key1))
    key_from1 = swapped(key1, 1)
    total = sent_to_all(piece[: tail // dp].astype(BF), "dp").reshape(tail, units)
    wo_total = piece[tail // dp :].reshape(head // 4, -1)

    tl = 512
    rows = spec((tl, width), lambda i: (i, 0))
    cols2 = spec((2, tl), lambda i: (0, i))
    pair_rows = spec((tl, 2 * head), lambda i: (i, 0))
    normed_grad, *last = pl.pallas_call(
        functools.partial(last_kernel, head=head, experts=experts),
        grid=(tokens // tl,),
        in_specs=[SMEM, spec((2, head, tl), lambda i: (0, 0, i)), pair_rows, pair_rows, pair_rows, pair_rows,
                  spec((16, tl), lambda i: (0, i)), cols2, rows, rows,
                  fixed((experts * head, width)), fixed((width, 2 * head)), fixed((2 * experts, width))],
        out_specs=[rows] + [fixed((share + 48, width))] * 4,
        out_shape=[shape((tokens, width), BF)] + [shape((share + 48, width), BF)] * 4,
        scratch_shapes=[
            pltpu.VMEM((experts * head, width), F32), pltpu.VMEM((2 * head, width), F32),
            pltpu.VMEM((8, width), F32),
        ],
        compiler_params=PARAMS,
        cost_estimate=cost(10),
    )(owners, q_grad, key0, key_from1, key_from2, key_from3, logit, routes_t, normed, x, wq,
      shared_proj, router_t)

    near, far = summed(last[0], swapped(last[1], 1)), summed(last[2], swapped(last[3], 1))
    from2 = swapped(far, 2)
    normed_grad, active, near = lax.optimization_barrier((normed_grad, active, near))
    to = 512
    rows = spec((to, width), lambda i: (i, 0))
    block_out, input_grad = pl.pallas_call(
        outputs_kernel,
        grid=(tokens // to,),
        in_specs=[spec((to, 4 * units), lambda i: (i, 0)), rows]
        + [spec((units, width), lambda i: (width // units, 0))] * 4
        + [fixed((1, width)), rows, rows, rows, fixed((1, width))],
        out_specs=[rows, rows],
        out_shape=[shape((tokens, width), BF), shape((tokens, width), F32)],
        compiler_params=PARAMS,
        cost_estimate=cost(10),
    )(active, middle, *feeds, reduce_bias[None].astype(F32), normed_grad, x, mid_grad, gain1)
    mine, total, input_grad = lax.optimization_barrier((summed(near, from2), total, input_grad))
    total = total.astype(F32)
    ends = jnp.broadcast_to(mine[share : share + 40][None], (dp, 40, width))
    each = jnp.concatenate([by_holder(mine[:share]), ends], axis=1)
    got = lax.all_to_all(each, "dp", split_axis=0, concat_axis=0, tiled=True)
    got = jnp.sum(got.astype(F32), axis=0)
    wq_total = got[: share // dp].reshape(head // 4, -1)
    ends = got[share // dp :]
    block = width // 4
    each = 2 * head // 4
    shared_total = jnp.concatenate(
        [ends[:each, g * block : (g + 1) * block] for g in range(4)], axis=0
    )
    cut = lax.dynamic_slice_in_dim(total[2 * width : 2 * width + 16], me * block, block, axis=1)
    return (
        block_out.reshape(1, tokens, width),
        input_grad.reshape(1, tokens, width),
        ends[each, :block],
        ends[each, block : 2 * block],
        cut[8 : 8 + experts].T,
        shared_total.T,
        wq_total,
        wo_total,
        cut[1],
        cut[2],
        total[:width],
        total[2 * width + 3],
        total[width : 2 * width].T,
        cut[0],
    )


def solution(mesh):
    both = P("dp", "mp", None)
    table = P("mp", "dp")
    placed = (
        both, both, P("dp"), P(), P(), P(), P(), table, table, P(), P(), P(None, "mp"), P("mp"),
        P("mp", None), P(), both,
    )
    given = (
        both, both, P("mp"), P("mp"), P("mp", None), P("mp", None), table, table, P("mp"), P("mp"),
        P(None, "mp"), P("mp"), P("mp", None), P("mp"),
    )
    return jax.shard_map(on_device, mesh=mesh, in_specs=placed, out_specs=given, check_vma=False)
```

```python
import functools

import jax
import jax.numpy as jnp
from jax import lax
from jax.experimental import pallas as pl
from jax.experimental.pallas import tpu as pltpu
from jax.sharding import PartitionSpec as P

F32 = jnp.float32
BF = jnp.bfloat16
EPS = 1e-05
SCALE = 0.125
TO_EXP2 = SCALE * 1.4426950408889634
MASKED = -1e30
GELU_A = 0.7978845608028654
GELU_B = 0.044715
SAFE = 60.0
LANES = 128


def nn(a, b):
    return lax.dot_general(a, b, (((1,), (0,)), ((), ())), preferred_element_type=F32)


def nt(a, b):
    return lax.dot_general(a, b, (((1,), (1,)), ((), ())), preferred_element_type=F32)


def tn(a, b):
    return lax.dot_general(a, b, (((0,), (0,)), ((), ())), preferred_element_type=F32)


def norm_parts(values):
    centred = values - jnp.mean(values, axis=-1, keepdims=True)
    inverse = lax.rsqrt(jnp.mean(centred * centred, axis=-1, keepdims=True) + EPS)
    return centred * inverse, inverse


def norm_back(grad, normal, inverse, gain):
    scaled = grad * gain
    return inverse * (
        scaled
        - jnp.mean(scaled, axis=-1, keepdims=True)
        - normal * jnp.mean(scaled * normal, axis=-1, keepdims=True)
    )


def three(value):
    high = value.astype(BF).astype(F32)
    rest = value - high
    middle = rest.astype(BF).astype(F32)
    return high, middle, rest - middle


def extra_rows(value, last):
    row = lax.broadcasted_iota(jnp.int32, (16, value.shape[1]), 0)
    high, middle, low = three(value)
    out = jnp.where(row == 0, -high, 0.0)
    out = jnp.where(row == 1, -middle, out)
    out = jnp.where(row == 2, -low, out)
    return jnp.where(row == 3, last, out)


def spread(first, second, route0, route1, experts):
    zero = jnp.zeros_like(first)
    return jnp.concatenate(
        [
            jnp.where(route0 == e, first, jnp.where(route1 == e, second, zero))
            for e in range(experts)
        ],
        axis=0,
    )


def picked(table, route, experts):
    head = table.shape[0] // experts
    out = jnp.zeros((head, table.shape[1]), F32)
    for e in range(experts):
        out = jnp.where(route == e, table[e * head : (e + 1) * head, :], out)
    return out


def key_rows(pair, live, head):
    lane = lax.broadcasted_iota(jnp.int32, pair.shape, 1)
    row = lax.broadcasted_iota(jnp.int32, pair.shape, 0)
    ones = jnp.where(lane < head + 3, 1.0, 0.0)
    mask = jnp.where(row < live, 0.0, MASKED)
    out = jnp.where(lane == head + 3, mask, ones)
    return jnp.where(lane < head, pair.astype(F32), out).astype(BF)


def first_kernel(x, gain, bias, router, proj, routes, normed, pairs, gates):
    experts = router.shape[0] // 2
    normal, _ = norm_parts(x[...].astype(F32))
    out = (normal * gain[...] + bias[...]).astype(BF)
    normed[...] = out
    pairs[...] = nn(out, proj[...]).astype(BF)
    logits = nt(router[...], out)
    route = routes[...]
    chosen = []
    for s in range(2):
        one = jnp.zeros((1, logits.shape[1]), F32)
        for e in range(experts):
            one = jnp.where(route[s : s + 1, :] == e, logits[e : e + 1, :], one)
        chosen.append(one)
    top = jnp.maximum(chosen[0], chosen[1])
    up0, up1 = jnp.exp(chosen[0] - top), jnp.exp(chosen[1] - top)
    inverse = 1.0 / (up0 + up1)
    gates[0:1, :] = up0 * inverse
    gates[1:2, :] = up1 * inverse


def query_kernel(normed, table, routes, queries, q_rows, *, experts):
    every = nt(table[...], normed[...])
    for s in range(2):
        one = picked(every, routes[s : s + 1, :], experts)
        queries[s] = one.astype(BF)
        q_rows[s] = jnp.concatenate([one, jnp.zeros_like(one)], axis=0).T.astype(BF)


def assembled(table, shares, where, experts, start):
    head = table.shape[0] // experts
    share = head // 4
    for o, part in enumerate(shares):
        for e in range(experts):
            at = pl.multiple_of(e * head + where[o] * share, share)
            here = slice(start + e * share, start + (e + 1) * share)
            table[pl.ds(at, share), :] = part[here, :]


def attend_kernel(where, length, q, p0, p1, p2, p3, out, kept, keys, values, limit, top, *, head, span):
    part = p0.shape[0]

    @pl.when((pl.program_id(0) == 0) & (pl.program_id(1) == 0))
    def _():
        row = lax.broadcasted_iota(jnp.int32, (LANES, LANES), 0)
        col = lax.broadcasted_iota(jnp.int32, (LANES, LANES), 1)
        move = jnp.where((col == row + head) & (row < head), 1.0, 0.0).astype(BF)
        count = jnp.where(row < head, 1.0, 0.0).astype(BF)
        longest = jnp.zeros((1, LANES), F32)
        for o, p in enumerate((p0, p1, p2, p3)):
            pair = p[...]
            live = length[0] - where[o] * part
            keys[o * part : (o + 1) * part, :] = key_rows(pair, live, head)
            turned = nt(move, pair)
            line = lax.broadcasted_iota(jnp.int32, turned.shape, 0)
            values[:, o * part : (o + 1) * part] = jnp.where(line == head, 1.0, turned).astype(BF)
            wide = pair.astype(F32)
            squares = nn((wide * wide).astype(BF), count)
            longest = jnp.maximum(longest, jnp.max(squares, axis=0, keepdims=True))
        limit[...] = jnp.broadcast_to(1.02 * jnp.sqrt(longest), limit.shape)

    query = q[0]
    wide = query.astype(F32)
    length = jnp.sqrt(jnp.sum(wide * wide, axis=0, keepdims=True))
    bound = length * limit[0:1, 0:1] * TO_EXP2
    top[...] = jnp.zeros_like(top)
    n = query.shape[1]
    rest = jnp.zeros((LANES - head - 16, n), BF)

    @pl.when(jnp.max(bound) > SAFE)
    def _():
        plain = jnp.concatenate(
            [query, extra_rows(jnp.zeros((1, n), F32), 1.0).astype(BF), rest], axis=0
        )

        def peak(j, now):
            at = pl.multiple_of(j * 512, 512)
            scores = nn(keys[pl.ds(at, 512), :], plain)
            return jnp.maximum(now, jnp.max(scores, axis=0, keepdims=True))

        best = lax.fori_loop(0, 4 * part // 512, peak, jnp.full((1, n), -3e38, F32))
        top[...] = jnp.broadcast_to(best, top.shape)

    extended = jnp.concatenate([query, extra_rows(top[0:1, :], 1.0).astype(BF), rest], axis=0)
    total = jnp.zeros((LANES, n), F32)
    for j in range(4 * part // span):
        here = slice(j * span, (j + 1) * span)
        weights = jnp.exp2(nn(keys[here, :], extended) * TO_EXP2).astype(BF)
        kept[here, :] = weights
        total = total + nn(values[:, here], weights)
    inverse = 1.0 / total[head : head + 1, :]
    out[0, 0:head, :] = total[0:head, :] * inverse
    out[0, head : head + 8, :] = jnp.broadcast_to(inverse, (8, n))


def attend_back_kernel(dot, do, q, *rest, head, places, first, carry):
    if not first:
        before, *rest = rest
    if carry:
        carried, *rest = rest
    pieces = len(places)
    weights, pairs, after = rest[:pieces], rest[pieces : 2 * pieces], rest[2 * pieces]
    grads = rest[2 * pieces + 1 : 3 * pieces + 1]
    values, turned, both = rest[3 * pieces + 1 :]
    step = pl.program_id(0)
    sizes = [pair.shape[0] for pair in pairs]
    spans = [slice(sum(sizes[:n]), sum(sizes[: n + 1])) for n in range(pieces)]

    @pl.when(step == 0)
    def _():
        row = lax.broadcasted_iota(jnp.int32, (head, LANES), 0)
        col = lax.broadcasted_iota(jnp.int32, (head, LANES), 1)
        same = jnp.where(row == col, 1.0, 0.0).astype(BF)
        for pair, here in zip(pairs, spans):
            rows = pair[...]
            turned[:, here] = nt(same, rows).astype(BF)
            lane = lax.broadcasted_iota(jnp.int32, rows.shape, 1)
            fixed = jnp.where(lane < 3, 1.0, 0.0)
            values[here, :] = jnp.where(lane < head, fixed, rows.astype(F32)).astype(BF)
        both[...] = jnp.zeros_like(both)

    right = jnp.concatenate([q[0], do[0]], axis=0)
    grown = jnp.zeros((head, q.shape[1]), F32)
    for weight, here in zip(weights, spans):
        attention = weight[...]
        scores = (attention.astype(F32) * nn(values[here, :], dot[0])).astype(BF)
        both[here, :] += nn(jnp.concatenate([scores, attention], axis=1), right)
        grown = grown + nn(turned[:, here], scores)
    after[0] = grown if first else before[0] + grown

    @pl.when(step == pl.num_programs(0) - 1)
    def _():
        for n, (grad, here) in enumerate(zip(grads, spans)):
            at = 0
            if carry and n == 0:
                at = carried.shape[0]
                grad[0:at, :] = carried[...]
            size = sizes[n]
            lane = lax.broadcasted_iota(jnp.int32, (size, LANES), 1)
            grad[at : at + size, :] = (both[here, :] * jnp.where(lane < head, SCALE, 1.0)).astype(BF)


def middle_kernel(
    where, att, routes, gates, x, up, normed,
    f0, f1, f2, f3, gain, bias,
    active, kept, mid_grad, do_rows, do_t, logit, g0, g1, g2, g3,
    we_sum, wr_sum, wo_sum, eb_sum, small, rt_sum, wo,
    *, head, experts,
):
    step = pl.program_id(0)

    @pl.when(step == 0)
    def _():
        for r in (we_sum, wr_sum, wo_sum, eb_sum, small, rt_sum):
            r[...] = jnp.zeros_like(r)
        assembled(wo, (f0, f1, f2, f3), where, experts, f0.shape[0] - experts * (head // 4))

    route0, route1 = routes[0:1, :], routes[1:2, :]
    gate0, gate1 = gates[0:1, :], gates[1:2, :]
    mix0, mix1 = att[0, 0:head, :], att[1, 0:head, :]
    low0, low1 = mix0.astype(BF).astype(F32), mix1.astype(BF).astype(F32)
    mixed = spread(gate0 * low0, gate1 * low1, route0, route1, experts).astype(BF)
    middle = x[...].astype(F32) + tn(mixed, wo[...])
    normal, inverse = norm_parts(middle)
    normed_two = (normal * gain[...] + bias[...]).astype(BF)
    upstream = up[...]
    n2t = normed_two.T
    upt = upstream.T
    ff = f0.shape[1]
    width = middle.shape[1]
    two_grad = jnp.zeros(middle.shape, F32)
    backs = []
    for o, f in enumerate((f0, f1, f2, f3)):
        here = slice(o * ff, (o + 1) * ff)
        v = nn(normed_two, f[0:width, :])
        v = v + f[width + ff : width + ff + 16, :].astype(F32)[0:1, :]
        square = v * v
        inner = v * (GELU_A + (GELU_A * GELU_B) * square)
        half = 0.5 + 0.5 * jnp.tanh(inner)
        act = v * half
        slope = half + act * (1.0 - half) * (2.0 * GELU_A + (6.0 * GELU_A * GELU_B) * square)
        active[:, here] = act.astype(BF)
        backs.append((nt(upstream, f[width : width + ff, :]) * slope).astype(BF))
    for o, f in enumerate((f0, f1, f2, f3)):
        here = slice(o * ff, (o + 1) * ff)
        back = backs[o]
        two_grad = two_grad + nt(back, f[0:width, :])
        we_sum[:, here] += nn(n2t, back)
        wr_sum[:, here] += nn(upt, active[:, here])
        eb_sum[0:1, here] += jnp.sum(back.astype(F32), axis=0, keepdims=True)
    kept[...] = middle.astype(BF)
    wide_up = upstream.astype(F32)
    mid = wide_up + norm_back(two_grad, normal, inverse, gain[...])
    mid_grad[...] = mid.astype(BF)
    small[0:1, :] += jnp.sum(wide_up, axis=0, keepdims=True)
    small[1:2, :] += jnp.sum(two_grad * normal, axis=0, keepdims=True)
    small[2:3, :] += jnp.sum(two_grad, axis=0, keepdims=True)
    mid_low = mid.astype(BF)
    wo_sum[...] += nn(mixed, mid_low)
    every = nt(wo[...], mid_low)
    pull0, pull1 = picked(every, route0, experts), picked(every, route1, experts)
    gate_grad0 = jnp.sum(low0 * pull0, axis=0, keepdims=True)
    gate_grad1 = jnp.sum(low1 * pull1, axis=0, keepdims=True)
    both = gate0 * gate_grad0 + gate1 * gate_grad1
    chosen0, chosen1 = gate0 * (gate_grad0 - both), gate1 * (gate_grad1 - both)
    row = lax.broadcasted_iota(jnp.int32, (16, chosen0.shape[1]), 0)
    logit_rows = jnp.where(row == route0, chosen0, jnp.where(row == route1, chosen1, 0.0))
    logit_high = logit_rows.astype(BF)
    logit_low = (logit_rows - logit_high.astype(F32)).astype(BF)
    logit[...] = logit_high
    here_normed = normed[...]
    rt_sum[...] += nn(logit_high, here_normed) + nn(logit_low, here_normed)
    rest = jnp.zeros((LANES - head - 16, row.shape[1]), F32)
    for s, (gate, pull, mix) in enumerate(((gate0, pull0, mix0), (gate1, pull1, mix1))):
        low = (gate * pull * att[s, head : head + 1, :]).astype(BF)
        grad = low.astype(F32)
        delta = jnp.sum(grad * mix, axis=0, keepdims=True)
        do_t[s] = jnp.concatenate([extra_rows(delta, 0.0), rest, grad], axis=0).astype(BF)
        do_rows[s] = jnp.concatenate([jnp.zeros_like(grad), grad], axis=0).T.astype(BF)

    @pl.when(step == pl.num_programs(0) - 1)
    def _():
        share = head // 4
        table = g0.shape[0] - experts * share
        for o, g in enumerate((g0, g1, g2, g3)):
            here = slice(o * ff, (o + 1) * ff)
            g[0:width, :] = we_sum[:, here].astype(BF)
            g[width : 2 * width, :] = wr_sum[:, here].astype(BF)
            line = lax.broadcasted_iota(jnp.int32, (8, ff), 0)
            head_rows = jnp.where(line == 3, eb_sum[0:1, here], small[...])
            g[2 * width : 2 * width + 16, :] = jnp.concatenate(
                [head_rows, rt_sum[0:8, :]], axis=0
            ).astype(BF)
            g[2 * width + 16 : table, :] = jnp.zeros((table - 2 * width - 16, ff), BF)
            for e in range(experts):
                at = pl.multiple_of(e * head + where[o] * share, share)
                g[table + e * share : table + (e + 1) * share, :] = wo_sum[
                    pl.ds(at, share), :
                ].astype(BF)


def last_kernel(
    where, dq, p0, p1, p2, p3, logit, routes, normed, x, wq, proj, router,
    out, s0, s1, s2, s3, wq_sum, sp_sum, small, turned, *, head, experts,
):
    step = pl.program_id(0)

    @pl.when(step == 0)
    def _():
        for r in (wq_sum, sp_sum, small):
            r[...] = jnp.zeros_like(r)

    route0, route1 = routes[0:1, :], routes[1:2, :]
    grad0, grad1 = dq[0] * SCALE, dq[1] * SCALE
    placed = spread(grad0, grad1, route0, route1, experts).astype(BF)
    own = p0[...].astype(F32)
    for p in (p1, p2, p3):
        own = own + p[...].astype(F32)
    pair = own.astype(BF)
    normed_grad = tn(placed, wq[...]) + nt(pair, proj[...]) + tn(logit[...], router[...])
    here_normed = normed[...]
    wq_sum[...] += nn(placed, here_normed)
    sp_sum[...] += tn(pair, here_normed)
    normal, _ = norm_parts(x[...].astype(F32))
    out[...] = normed_grad.astype(BF)
    small[0:1, :] += jnp.sum(normed_grad * normal, axis=0, keepdims=True)
    small[1:2, :] += jnp.sum(normed_grad, axis=0, keepdims=True)

    @pl.when(step == pl.num_programs(0) - 1)
    def _():
        share = head // 4
        block = sp_sum.shape[1] // 4
        each = sp_sum.shape[0] // 4
        table = experts * share
        turned[...] = sp_sum[...].T
        for o, s in enumerate((s0, s1, s2, s3)):
            owner = where[o]
            for e in range(experts):
                at = pl.multiple_of(e * head + owner * share, share)
                s[e * share : (e + 1) * share, :] = wq_sum[pl.ds(at, share), :].astype(BF)
            lanes = pl.ds(pl.multiple_of(owner * block, block), block)
            s[table + each : table + each + 16, :] = jnp.zeros((16, 4 * block), BF)
            line = lax.broadcasted_iota(jnp.int32, (16, block), 0)
            for g in range(2):
                ends = jnp.where(line == 0, small[g : g + 1, lanes], 0.0)
                s[table + each : table + each + 16, g * block : (g + 1) * block] = ends.astype(BF)
            for g in range(4):
                piece = turned[pl.ds(pl.multiple_of(owner * block + g * each, each), each), :]
                s[table : table + each, g * block : (g + 1) * block] = piece.astype(BF)


def outputs_kernel(active, middle, r0, r1, r2, r3, rb, normed_grad, x, mid_grad, gain, out, x_grad):
    ff = r0.shape[0]
    total = middle[...].astype(F32) + rb[...]
    for o, r in enumerate((r0, r1, r2, r3)):
        total = total + nn(active[:, o * ff : (o + 1) * ff], r[...])
    out[...] = total.astype(BF)
    normal, inverse = norm_parts(x[...].astype(F32))
    back = norm_back(normed_grad[...].astype(F32), normal, inverse, gain[...])
    x_grad[...] = mid_grad[...].astype(F32) + back


def swapped(value, bit):
    return lax.ppermute(value, "mp", [(i, i ^ bit) for i in range(4)])


def four(value):
    across = swapped(value, 2)
    return value, swapped(value, 1), across, swapped(across, 1)


def summed(a, b):
    return (a.astype(F32) + b.astype(F32)).astype(BF)


def sent_to_all(value, axes):
    n = lax.axis_size(axes)
    wide = jnp.broadcast_to(value[None], (n,) + value.shape)
    return lax.all_to_all(wide, axes, split_axis=0, concat_axis=0, tiled=True)


def whole_table(share, experts):
    dp, mp = lax.axis_size("dp"), lax.axis_size("mp")
    rows, cols = share.shape
    every = sent_to_all(share, ("dp", "mp"))
    each = every.reshape(experts, dp // experts, mp, rows, cols)
    return each.transpose(0, 2, 3, 1, 4).reshape(experts * mp * rows, dp // experts * cols)


def spec(shape, index):
    return pl.BlockSpec(shape, index)


def fixed(shape):
    return pl.BlockSpec(shape, lambda *_: (0,) * len(shape))


def shape(dims, kind):
    return jax.ShapeDtypeStruct(dims, kind)


SMEM = pl.BlockSpec(memory_space=pltpu.SMEM)
PARAMS = pltpu.CompilerParams(vmem_limit_bytes=58 * 2**20)


def cost(us):
    return pl.CostEstimate(flops=int(us * 1.1e9), bytes_accessed=1024, transcendentals=0)


def tied(value, *others):
    return lax.optimization_barrier((value, *others))[0]


def on_device(
    block_input, routes, lengths, first_gain, first_bias, router_weight, shared_proj,
    query_weight, output_weight, second_gain, second_bias, expand_weight, expand_bias,
    reduce_weight, reduce_bias, upstream_grad,
):
    tokens, width = block_input.shape[1], block_input.shape[2]
    experts = router_weight.shape[1]
    head = query_weight.shape[0] * lax.axis_size("mp")
    dp = lax.axis_size("dp")
    units = expand_weight.shape[1]
    me = lax.axis_index("mp")
    owners = me ^ jnp.arange(4, dtype=jnp.int32)
    x = block_input.reshape(tokens, width)
    up = upstream_grad.reshape(tokens, width)
    routes_t = routes.reshape(tokens, 2).T
    router_t = jnp.pad(router_weight.T, ((0, experts), (0, 0)))
    gain1, bias1 = first_gain[None], first_bias[None]
    gain2, bias2 = second_gain[None], second_bias[None]

    wq = whole_table(query_weight, experts)

    tb = 512
    rows = spec((tb, width), lambda i: (i, 0))
    cols2 = spec((2, tb), lambda i: (0, i))
    normed, pairs, gates = pl.pallas_call(
        first_kernel,
        grid=(tokens // tb,),
        in_specs=[rows, fixed((1, width)), fixed((1, width)), fixed((2 * experts, width)),
                  fixed((width, 2 * head)), cols2],
        out_specs=[rows, spec((tb, 2 * head), lambda i: (i, 0)), cols2],
        out_shape=[shape((tokens, width), BF), shape((tokens, 2 * head), BF), shape((2, tokens), F32)],
        compiler_params=PARAMS,
        cost_estimate=cost(5),
    )(x, gain1, bias1, router_t, shared_proj, routes_t)

    pair_across = swapped(pairs, 2)
    pair_beside = swapped(pairs, 1)
    output_weight, wq = lax.optimization_barrier((output_weight, wq))
    o_share = sent_to_all(output_weight, "dp")
    o_share = o_share.reshape(experts, dp // experts, head // 4, -1).transpose(0, 2, 1, 3)
    o_share = o_share.reshape(experts * head // 4, width)
    queries, q_rows = pl.pallas_call(
        functools.partial(query_kernel, experts=experts),
        grid=(tokens // tb,),
        in_specs=[rows, fixed((experts * head, width)), cols2],
        out_specs=[spec((2, head, tb), lambda i: (0, 0, i)), spec((2, tb, LANES), lambda i: (0, i, 0))],
        out_shape=[shape((2, head, tokens), BF), shape((2, tokens, LANES), BF)],
        compiler_params=PARAMS,
        cost_estimate=cost(5),
    )(normed, wq, routes_t)
    feed = jnp.concatenate(
        [expand_weight, reduce_weight, jnp.broadcast_to(expand_bias[None], (16, units)), o_share],
        axis=0,
    )
    feed, pair_across, queries = lax.optimization_barrier((feed, pair_across, queries))
    pair = (pairs, pair_beside, pair_across, swapped(pair_across, 1))
    feed_across = swapped(feed, 2)

    tq = 512
    att, kept = pl.pallas_call(
        functools.partial(attend_kernel, head=head, span=4 * tokens),
        grid=(2, tokens // tq),
        in_specs=[SMEM, SMEM, spec((1, head, tq), lambda s, i: (s, 0, i))] + [fixed((tokens, 2 * head))] * 4,
        out_specs=[spec((1, head + 8, tq), lambda s, i: (s, 0, i)),
                   spec((4 * tokens, tq), lambda s, i: (0, s * (tokens // tq) + i))],
        out_shape=[shape((2, head + 8, tokens), F32), shape((4 * tokens, 2 * tokens), BF)],
        scratch_shapes=[
            pltpu.VMEM((4 * tokens, LANES), BF), pltpu.VMEM((LANES, 4 * tokens), BF),
            pltpu.VMEM((8, LANES), F32), pltpu.VMEM((8, tq), F32),
        ],
        compiler_params=PARAMS,
        cost_estimate=cost(33),
    )(owners, lengths, queries, *pair)

    feed_across = tied(feed_across, att)
    feeds = (feed, swapped(feed, 1), feed_across, swapped(feed_across, 1))

    tm = 512
    rows = spec((tm, width), lambda i: (i, 0))
    cols2 = spec((2, tm), lambda i: (0, i))
    tail = 2 * width + 64
    share = experts * head // 4
    slot = tail + share
    both_rows = spec((2, tm, LANES), lambda i: (0, i, 0))
    both_cols = spec((2, LANES, tm), lambda i: (0, 0, i))
    att_cols = spec((2, head + 8, tm), lambda i: (0, 0, i))
    active, middle, mid_grad, do_rows, do_t, logit, *ffn = pl.pallas_call(
        functools.partial(middle_kernel, head=head, experts=experts),
        grid=(tokens // tm,),
        in_specs=[SMEM, att_cols, cols2, cols2, rows, rows, rows]
        + [fixed(feed.shape)] * 4 + [fixed((1, width))] * 2,
        out_specs=[spec((tm, 4 * units), lambda i: (i, 0)), rows, rows, both_rows, both_cols, spec((16, tm), lambda i: (0, i))]
        + [fixed((slot, units))] * 4,
        out_shape=[shape((tokens, 4 * units), BF), shape((tokens, width), BF), shape((tokens, width), BF),
                   shape((2, tokens, LANES), BF), shape((2, LANES, tokens), BF), shape((16, tokens), BF)]
        + [shape((slot, units), BF)] * 4,
        scratch_shapes=[
            pltpu.VMEM((width, 4 * units), F32), pltpu.VMEM((width, 4 * units), F32),
            pltpu.VMEM((experts * head, width), F32), pltpu.VMEM((8, 4 * units), F32),
            pltpu.VMEM((8, width), F32), pltpu.VMEM((16, width), F32),
            pltpu.VMEM((experts * head, width), BF),
        ],
        compiler_params=PARAMS,
        cost_estimate=cost(50),
    )(owners, att, routes_t, gates, x, up, normed, *feeds, gain2, bias2)

    half = tokens // 2

    def back_call(places, before, us, carried=None):
        carry = carried is not None
        ends = [size for _, _, size in places]
        ends[0] += carried.shape[0] if carry else 0
        many = sum(size for _, _, size in places)
        first = before is None
        tq = half if many <= half else 512
        per = tokens // tq
        row_block = spec((1, tq, LANES), lambda i: (i // per, i % per, 0))
        col_block = spec((1, LANES, tq), lambda i: (i // per, 0, i % per))
        grad_block = spec((1, head, tq), lambda i: (i // per, 0, i % per))
        return pl.pallas_call(
            functools.partial(attend_back_kernel, head=head, places=places, first=first, carry=carry),
            grid=(2 * per,),
            in_specs=[col_block, row_block, row_block] + [grad_block] * (not first)
            + [fixed(carried.shape) for _ in range(carry)]
            + [spec((size, tq), lambda i, at=o * tokens // size + at: (at, i)) for o, at, size in places]
            + [spec((size, 2 * head), lambda i, at=at: (at, 0)) for _, at, size in places],
            out_specs=[grad_block] + [fixed((size, 2 * head)) for size in ends],
            out_shape=[shape((2, head, tokens), F32)]
            + [shape((size, 2 * head), BF) for size in ends],
            input_output_aliases={} if first else {3: 0},
            scratch_shapes=[
                pltpu.VMEM((many, LANES), BF), pltpu.VMEM((head, many), BF),
                pltpu.VMEM((many, LANES), F32),
            ],
            compiler_params=PARAMS,
            cost_estimate=cost(us),
        )(do_t, do_rows, q_rows, *([] if first else [before]), *([carried] if carry else []), *[kept] * len(places),
          *[pair[o] for o, _, _ in places])

    def by_holder(rows_of):
        each = rows_of.reshape(experts, head // 4, dp // experts, -1).transpose(0, 2, 1, 3)
        return each.reshape(dp, -1, width)

    from3, from1 = swapped(ffn[3], 1), swapped(ffn[1], 1)
    q_grad, key3a = back_call([(3, 0, half)], None, 11)
    far, near = summed(ffn[2], from3), summed(ffn[0], from1)
    q_grad, far, near = lax.optimization_barrier((q_grad, far, near))
    from2 = swapped(far, 2)
    q_grad, key3, key2 = back_call([(3, 1, half), (2, 0, tokens)], q_grad, 30, key3a)
    own = summed(near, from2)
    own = jnp.concatenate([own[:tail].reshape(dp, -1, width), by_holder(own[tail:])], axis=1)
    q_grad, own, key3, key2 = lax.optimization_barrier((q_grad, own, key3, key2))
    arrived = lax.all_to_all(own, "dp", split_axis=0, concat_axis=0, tiled=True)
    key_from3, key_from2 = swapped(key3, 3), swapped(key2, 2)
    q_grad, key1, key0 = back_call([(1, 0, tokens), (0, 0, tokens)], q_grad, 39)
    piece = jnp.sum(arrived.astype(F32), axis=0)
    q_grad, piece, key1 = lax.optimization_barrier((q_grad, piece, key1))
    key_from1 = swapped(key1, 1)
    total = sent_to_all(piece[: tail // dp].astype(BF), "dp").reshape(tail, units)
    wo_total = piece[tail // dp :].reshape(head // 4, -1)

    tl = 512
    rows = spec((tl, width), lambda i: (i, 0))
    cols2 = spec((2, tl), lambda i: (0, i))
    pair_rows = spec((tl, 2 * head), lambda i: (i, 0))
    normed_grad, *last = pl.pallas_call(
        functools.partial(last_kernel, head=head, experts=experts),
        grid=(tokens // tl,),
        in_specs=[SMEM, spec((2, head, tl), lambda i: (0, 0, i)), pair_rows, pair_rows, pair_rows, pair_rows,
                  spec((16, tl), lambda i: (0, i)), cols2, rows, rows,
                  fixed((experts * head, width)), fixed((width, 2 * head)), fixed((2 * experts, width))],
        out_specs=[rows] + [fixed((share + 48, width))] * 4,
        out_shape=[shape((tokens, width), BF)] + [shape((share + 48, width), BF)] * 4,
        scratch_shapes=[
            pltpu.VMEM((experts * head, width), F32), pltpu.VMEM((2 * head, width), F32),
            pltpu.VMEM((8, width), F32), pltpu.VMEM((width, 2 * head), F32),
        ],
        compiler_params=PARAMS,
        cost_estimate=cost(10),
    )(owners, q_grad, key0, key_from1, key_from2, key_from3, logit, routes_t, normed, x, wq,
      shared_proj, router_t)

    near, far = summed(last[0], swapped(last[1], 1)), summed(last[2], swapped(last[3], 1))
    from2 = swapped(far, 2)
    normed_grad, active, near = lax.optimization_barrier((normed_grad, active, near))
    to = 512
    rows = spec((to, width), lambda i: (i, 0))
    block_out, input_grad = pl.pallas_call(
        outputs_kernel,
        grid=(tokens // to,),
        in_specs=[spec((to, 4 * units), lambda i: (i, 0)), rows]
        + [spec((units, width), lambda i: (width // units, 0))] * 4
        + [fixed((1, width)), rows, rows, rows, fixed((1, width))],
        out_specs=[rows, rows],
        out_shape=[shape((tokens, width), BF), shape((tokens, width), F32)],
        compiler_params=PARAMS,
        cost_estimate=cost(10),
    )(active, middle, *feeds, reduce_bias[None].astype(F32), normed_grad, x, mid_grad, gain1)
    mine, total, input_grad = lax.optimization_barrier((summed(near, from2), total, input_grad))
    total = total.astype(F32)
    ends = jnp.broadcast_to(mine[share : share + 40][None], (dp, 40, width))
    each = jnp.concatenate([by_holder(mine[:share]), ends], axis=1)
    got = lax.all_to_all(each, "dp", split_axis=0, concat_axis=0, tiled=True)
    got = jnp.sum(got.astype(F32), axis=0)
    wq_total = got[: share // dp].reshape(head // 4, -1)
    ends = got[share // dp :]
    block = width // 4
    each = 2 * head // 4
    shared_total = jnp.concatenate(
        [ends[:each, g * block : (g + 1) * block] for g in range(4)], axis=0
    )
    cut = lax.dynamic_slice_in_dim(total[2 * width : 2 * width + 16], me * block, block, axis=1)
    return (
        block_out.reshape(1, tokens, width),
        input_grad.reshape(1, tokens, width),
        ends[each, :block],
        ends[each, block : 2 * block],
        cut[8 : 8 + experts].T,
        shared_total,
        wq_total,
        wo_total,
        cut[1],
        cut[2],
        total[:width],
        total[2 * width + 3],
        total[width : 2 * width].T,
        cut[0],
    )


def solution(mesh):
    both = P("dp", "mp", None)
    table = P("mp", "dp")
    placed = (
        both, both, P("dp"), P(), P(), P(), P(), table, table, P(), P(), P(None, "mp"), P("mp"),
        P("mp", None), P(), both,
    )
    given = (
        both, both, P("mp"), P("mp"), P("mp", None), P("mp", None), table, table, P("mp"), P("mp"),
        P(None, "mp"), P("mp"), P("mp", None), P("mp"),
    )
    return jax.shard_map(on_device, mesh=mesh, in_specs=placed, out_specs=given, check_vma=False)
```
